32 devices in a mesh: groups: 2 (over y), wide: 4 (over z), node: 4 (over x, core).
Axes of the slice: x: 2, y: 2, z: 4, core: 2. Of those that a mesh axis runs over, the one named last changes fastest.
Arguments:
- tokens: bfloat16 [1024, 2304], P(('groups', 'wide')), parts along dimension 0, may hold values from -6 to 6
- cotangent: bfloat16 [1024, 2304], P(('groups', 'wide')), parts along dimension 0, may hold values from -1.5 to 1.5
- tiles: bfloat16 [4, 4, 25, 128, 128], P('node', 'wide'), may hold values from -0.125 to 0.125
- tile_ids: int32 [4, 4, 25], P('node', 'wide'), may hold values from 0 to 215, as said below
- tile_counts: int32 [4, 4], P('node', 'wide'), may hold values from 0 to 25, as said below
Outputs:
- mixed: bfloat16 [1024, 2304], P(('groups', 'wide')), parts along dimension 0
- input_grad: bfloat16 [1024, 2304], P(('groups', 'wide')), parts along dimension 0
- grad_tiles: bfloat16 [8, 4, 25, 128, 128], P(('groups', 'node'), 'wide'), parts along dimension 0
The draws below stay inside these ranges and needn't reach their ends.
There are 2 independent parts, one for each index of `groups`. The reference program is written for one: setup_inputs(seed, part) draws one part's arguments, and reference() takes and returns one part's arrays. A program takes and returns all parts, laid end to end along the dimension named above; an argument that names none is the same for every part. Nothing has to cross between parts.
Inputs may be any that keep to these rules, and one draw needn't show every extreme that they name: `tile_ids`: for each index of node, the live slots of all indices of wide name 97 different blocks; slots that are not live hold any block number. `tile_counts`: for each index of node the counts sum to 97.
All inputs are finite; a program needn't handle non-finite values.
Results may differ from the reference program's by a relative error of at most 0.0095.
Values may be sent and summed in bfloat16 or wider, within the bound.
A program may use at most 64 MiB of HBM per device.

```python
import math
import jax
import jax.numpy as jnp
from jax import lax

D = 2304
FF_DEV = 512
BLK = 128
TOK_DEV = 128
TOKENS = 512
NBLK = 216
KEPT = 97
SLOTS = 25
N_WIDE = 4
N_NODE = 4


def slot_layout(key):

    def one_slice(slice_key):
        key_kept, key_full, key_order, key_filler = jax.random.split(slice_key, 4)
        kept = jax.random.permutation(key_kept, NBLK)[:KEPT].astype(jnp.int32)
        full_owner = jax.random.randint(key_full, (), 0, N_WIDE)
        order = jax.random.permutation(key_order, N_WIDE * SLOTS).astype(jnp.int32)
        owner = jnp.arange(N_WIDE * SLOTS, dtype=jnp.int32) // SLOTS
        scores = order + jnp.where(owner == full_owner, 0, N_WIDE * SLOTS).astype(jnp.int32)
        ranking = jnp.argsort(jnp.argsort(scores, stable=True), stable=True)
        occupied = (ranking < KEPT).reshape(N_WIDE, SLOTS)
        counts = jnp.sum(occupied.astype(jnp.int32), axis=1).astype(jnp.int32)
        offsets = jnp.cumsum(counts) - counts
        slot_index = jnp.arange(SLOTS, dtype=jnp.int32)
        live_slots = slot_index[None, :] < counts[:, None]
        position = jnp.clip(offsets[:, None] + slot_index[None, :], 0, KEPT - 1)
        filler = jax.random.randint(key_filler, (N_WIDE, SLOTS), 0, NBLK).astype(jnp.int32)
        block_ids = jnp.where(live_slots, kept[position], filler).astype(jnp.int32)
        return (block_ids, counts)
    slice_keys = jax.random.split(key, N_NODE)
    return jax.vmap(one_slice)(slice_keys)


def draw_tile_ids(key, part):
    return slot_layout(key)[0]


def draw_tile_counts(key, part):
    return slot_layout(key)[1]


def block_levels(key, shape, shards, smallest, high):
    loudness = 1.0
    for dim, blocks in shards:
        steps = jax.random.uniform(jax.random.fold_in(jax.random.fold_in(key, 6), dim), (blocks,), jnp.float32, smallest / len(shards), high / len(shards))
        loudness = loudness * jnp.repeat(jnp.exp(steps), shape[dim] // blocks).reshape((-1,) + (1,) * (len(shape) - 1 - dim))
    return loudness


def noise(key, shape, scale, limit, cuts=(), held_as=jnp.bfloat16):
    values = scale * jax.random.normal(key, shape, jnp.float32)
    if cuts:
        values = values * block_levels(key, shape, cuts, -0.22, 0.18)
    return jnp.clip(values, -limit, limit).astype(held_as)


def setup_inputs(seed: int = 0, part: int = 0) -> dict:
    key_of = jax.random.split(jax.random.key(seed), 6)
    part_splits = jax.random.split(jax.random.fold_in(key_of[5], part), 6)
    return {
        "tokens": noise(part_splits[0], (TOKENS, D), 1.0, 6.0, ((0, 4),)),
        "cotangent": noise(part_splits[1], (TOKENS, D), 0.25, 1.5, ((0, 4),)),
        "tiles": noise(key_of[2], (N_NODE, N_WIDE, SLOTS, BLK, BLK), D ** -0.5, 0.125, ((0, 4), (1, 4))),
        "tile_ids": draw_tile_ids(jax.random.fold_in(key_of[5], 71), part),
        "tile_counts": draw_tile_counts(jax.random.fold_in(key_of[5], 71), part),
    }


gelu_scale = math.sqrt(2.0 / math.pi)
cubic_term = 0.044715

def gelu_parts(pre):
    tangent = jnp.tanh(gelu_scale * (pre + cubic_term * pre * pre * pre))
    value = 0.5 * pre * (1.0 + tangent)
    slope = 0.5 * (1.0 + tangent) + 0.5 * pre * (1.0 - tangent * tangent) * gelu_scale * (1.0 + 3.0 * cubic_term * pre * pre)
    return (value, slope)

def contract_rows(left, right):
    return lax.dot_general(left, right, (((1,), (1,)), ((), ())), preferred_element_type=jnp.float32)

def contract_tokens(left, right):
    return lax.dot_general(left, right, (((0,), (0,)), ((), ())), preferred_element_type=jnp.float32)

def reference(tokens, cotangent, tiles, tile_ids, tile_counts):
    row_blocks = D // BLK
    col_blocks = FF_DEV // BLK
    slot_index = jnp.arange(SLOTS, dtype=jnp.int32)
    live_slots = slot_index[None, None, :] < tile_counts[:, :, None]
    targets = jnp.where(live_slots, tile_ids, NBLK).astype(jnp.int32)

    def one_slice(node_index):
        blocks = jnp.zeros((NBLK + 1, BLK, BLK), jnp.bfloat16)
        blocks = blocks.at[targets[node_index].reshape(-1)].set(tiles[node_index].reshape(-1, BLK, BLK))
        weights = blocks[:NBLK].reshape(3, row_blocks, col_blocks, BLK, BLK).transpose(0, 1, 3, 2, 4).reshape(3, D, FF_DEV)
        gate_pre = jnp.dot(tokens, weights[0], preferred_element_type=jnp.float32)
        up_pre = jnp.dot(tokens, weights[1], preferred_element_type=jnp.float32)
        value, slope = gelu_parts(gate_pre)
        hidden = (value * up_pre).astype(jnp.bfloat16)
        out_part = contract_rows(hidden, weights[2]).astype(jnp.bfloat16)
        hidden_grad = jnp.dot(cotangent, weights[2], preferred_element_type=jnp.float32)
        gate_grad = (hidden_grad * up_pre * slope).astype(jnp.bfloat16)
        up_grad = (hidden_grad * value).astype(jnp.bfloat16)
        input_part = (contract_rows(gate_grad, weights[0]) + contract_rows(up_grad, weights[1])).astype(jnp.bfloat16)

        def accumulate(totals, member):
            rows_in, rows_gate, rows_up, rows_out, rows_hidden = member
            terms = jnp.stack([contract_tokens(rows_in, rows_gate), contract_tokens(rows_in, rows_up), contract_tokens(rows_out, rows_hidden)])
            rounded = lax.optimization_barrier(terms.astype(jnp.bfloat16))
            return (totals + rounded.astype(jnp.float32), None)
        members = tuple((array.reshape(N_WIDE, TOK_DEV, array.shape[1]) for array in (tokens, gate_grad, up_grad, cotangent, hidden)))
        sums, _ = lax.scan(accumulate, jnp.zeros((3, D, FF_DEV), jnp.float32), members)
        grad_blocks = sums.reshape(3, row_blocks, BLK, col_blocks, BLK).transpose(0, 1, 3, 2, 4).reshape(NBLK, BLK, BLK)
        picked = grad_blocks[tile_ids[node_index].astype(jnp.int32)]
        picked = jnp.where(live_slots[node_index][:, :, None, None], picked, jnp.float32(0.0))
        return (out_part, input_part, picked.astype(jnp.bfloat16))
    out_parts, input_parts, grad_tiles = lax.map(one_slice, jnp.arange(N_NODE, dtype=jnp.int32))
    mixed = lax.optimization_barrier(jnp.sum(out_parts.astype(jnp.float32), axis=0)).astype(jnp.bfloat16)
    input_grad = lax.optimization_barrier(jnp.sum(input_parts.astype(jnp.float32), axis=0)).astype(jnp.bfloat16)
    return (mixed, input_grad, grad_tiles)
```

```python
import functools
import math

import jax
import jax.numpy as jnp
from jax import lax
from jax.experimental import pallas as pl
from jax.experimental.pallas import tpu as pltpu
from jax.sharding import PartitionSpec as P

FF_DEV = 512
NBLK = 216
EDGE = 128
COLS = FF_DEV // EDGE
MESH = pl.DeviceIdType.MESH

gelu_scale = math.sqrt(2.0 / math.pi)
cubic_term = 0.044715


def gelu_parts(pre):
    tangent = jnp.tanh(gelu_scale * (pre + cubic_term * pre * pre * pre))
    value = 0.5 * pre * (1.0 + tangent)
    slope = 0.5 * (1.0 + tangent) + 0.5 * pre * (1.0 - tangent * tangent) * gelu_scale * (
        1.0 + 3.0 * cubic_term * pre * pre
    )
    return (value, slope)


def contract_rows(left, right):
    return lax.dot_general(
        left, right, (((1,), (1,)), ((), ())), preferred_element_type=jnp.float32
    )


def contract_tokens(left, right):
    return lax.dot_general(
        left, right, (((0,), (0,)), ((), ())), preferred_element_type=jnp.float32
    )


def remote(src, dst, send, recv, where):
    return pltpu.make_async_remote_copy(
        src_ref=src, dst_ref=dst, send_sem=send, recv_sem=recv, device_id=where, device_id_type=MESH
    )


def gather_kernel(n_wide, chunks, tiles_ref, ids_ref, all_ref, allids_ref,
                  zsend, zrecv, ysend, yrecv, isend, irecv, own_sem):
    w = lax.axis_index("wide")
    g = lax.axis_index("groups")
    other = 1 - g
    rows = tiles_ref.shape[0]
    half = rows // 2
    step = half // chunks

    barrier = pltpu.get_barrier_semaphore()
    for d in range(1, n_wide):
        pl.semaphore_signal(barrier, inc=1, device_id={"wide": lax.rem(w + d, n_wide)}, device_id_type=MESH)
    pl.semaphore_signal(barrier, inc=1, device_id={"groups": other}, device_id_type=MESH)
    own = pltpu.make_async_copy(tiles_ref, all_ref.at[pl.ds(pl.multiple_of(w * rows, 16), rows)], own_sem)
    own.start()
    all_ref[n_wide * rows:, :] = jnp.zeros((EDGE, EDGE), all_ref.dtype)
    allids_ref[w] = ids_ref[...]
    pl.semaphore_wait(barrier, n_wide)

    def part(group, k):
        return pl.ds(pl.multiple_of(group * half + k * step, 16), step)

    def piece(j, group, k):
        return all_ref.at[pl.ds(pl.multiple_of(j * rows + group * half + k * step, 16), step)]

    def z_copy(j, k, way):
        return remote(
            piece(j, g, k), piece(j, g, k),
            zsend.at[0 if way > 0 else 1, j, k], zrecv.at[j, k], {"wide": w + way},
        )

    def z_own(k, way):
        return remote(
            tiles_ref.at[part(g, k)], piece(w, g, k),
            zsend.at[0 if way > 0 else 1, w, k], zrecv.at[w, k], {"wide": w + way},
        )

    def y_copy(j, k, group):
        return remote(
            piece(j, group, k), piece(j, group, k),
            ysend.at[j, k], yrecv.at[j, k], {"groups": other},
        )

    def ids_copy(d):
        to = lax.rem(w + d, n_wide)
        return remote(allids_ref.at[w], allids_ref.at[w], isend.at[d], irecv.at[w], {"wide": to})

    right = w < n_wide - 1
    left = w > 0
    for k in range(chunks):
        @pl.when(right)
        def _():
            z_own(k, 1).start()

        @pl.when(left)
        def _():
            z_own(k, -1).start()
    for d in range(1, n_wide):
        ids_copy(d).start()
    for d in range(1, n_wide):
        for k in range(chunks):
            for way in (1, -1):
                j = w - d * way
                have = (j >= 0) if way > 0 else (j < n_wide)

                @pl.when(have)
                def _():
                    z_copy(j, k, way).wait_recv()

                @pl.when(have & (right if way > 0 else left))
                def _():
                    z_copy(j, k, way).start()

                @pl.when(have)
                def _():
                    y_copy(j, k, g).start()
    own.wait()
    for k in range(chunks):
        @pl.when(right)
        def _():
            z_own(k, 1).wait_send()

        @pl.when(left)
        def _():
            z_own(k, -1).wait_send()
    for d in range(1, n_wide):
        ids_copy(d).wait_send()
        j = lax.rem(w + d, n_wide)
        remote(allids_ref.at[j], allids_ref.at[j], isend.at[d], irecv.at[j], {"wide": j}).wait_recv()
        for k in range(chunks):
            y_copy(j, k, g).wait_send()
            y_copy(j, k, other).wait_recv()
            for way in (1, -1):
                i = w - d * way
                have = (i >= 0) if way > 0 else (i < n_wide)

                @pl.when(have & (right if way > 0 else left))
                def _():
                    z_copy(i, k, way).wait_send()


def gather_tiles(tiles, ids, n_wide):
    rows = tiles.shape[0]
    chunks = 5 if (rows // 2) % 80 == 0 else 1
    dma = pltpu.SemaphoreType.DMA
    vmem = pl.BlockSpec(memory_space=pltpu.VMEM)
    return pl.pallas_call(
        functools.partial(gather_kernel, n_wide, chunks),
        out_shape=(
            jax.ShapeDtypeStruct((n_wide * rows + EDGE, EDGE), tiles.dtype),
            jax.ShapeDtypeStruct((n_wide,) + ids.shape, ids.dtype),
        ),
        in_specs=[vmem, vmem],
        out_specs=(vmem, vmem),
        scratch_shapes=[
            dma((2, n_wide, chunks)), dma((n_wide, chunks)), dma((n_wide, chunks)), dma((n_wide, chunks)),
            dma((n_wide,)), dma((n_wide,)), dma,
        ],
        compiler_params=pltpu.CompilerParams(
            collective_id=0, has_side_effects=True, vmem_limit_bytes=40 << 20
        ),
    )(tiles, ids)


def main_kernel(n_wide, n_node,
                inv_ref, tok_ref, cot_ref, tiles_ref,
                mixed_ref, input_ref, gath_ref, acts_ref,
                weights, acts, parts, arrived,
                xsend, xrecv, nsend, nrecv, hsend, hrecv, psend, precv, osend, orecv, ssem):
    w = lax.axis_index("wide")
    n = lax.axis_index("node")
    toks, width = tok_ref.shape
    piece = toks // n_node
    rblocks = width // EDGE
    per = rblocks * COLS
    bits = n_node.bit_length() - 1

    barrier = pltpu.get_barrier_semaphore()
    for d in range(1, n_wide):
        pl.semaphore_signal(barrier, inc=1, device_id={"wide": lax.rem(w + d, n_wide)}, device_id_type=MESH)
    for d in range(1, n_node):
        pl.semaphore_signal(barrier, inc=1, device_id={"node": lax.rem(n + d, n_node)}, device_id_type=MESH)

    def rows_of(j, q):
        return pl.ds(pl.multiple_of(j * toks + q * piece, 16), piece)

    own_rows = pl.ds(pl.multiple_of(w * toks, 16), toks)
    def keep(t):
        return pltpu.make_async_copy((tok_ref, cot_ref)[t], gath_ref.at[t, own_rows, :], ssem.at[t])

    keep(0).start()
    keep(1).start()
    pl.semaphore_wait(barrier, n_wide + n_node - 2)

    def x_copy(j, d, t):
        mine = (tok_ref, cot_ref)[t].at[pl.ds(pl.multiple_of(n * piece, 16), piece), :]
        return remote(
            mine, gath_ref.at[t, rows_of(j, n), :], xsend.at[d, t], xrecv.at[j, t],
            {"wide": lax.rem(w + d, n_wide)},
        )

    for d in range(1, n_wide):
        for t in range(2):
            x_copy(w, d, t).start()

    def place(r, _):
        for m in range(3):
            for c in range(COLS):
                i = inv_ref[m * per + r * COLS + c]
                weights[m, pl.ds(pl.multiple_of(r * EDGE, EDGE), EDGE), c * EDGE:(c + 1) * EDGE] = tiles_ref[i]
        return 0

    lax.fori_loop(0, rblocks, place, 0)

    gate = jnp.dot(tok_ref[...], weights[0], preferred_element_type=jnp.float32)
    up = jnp.dot(tok_ref[...], weights[1], preferred_element_type=jnp.float32)
    value, slope = gelu_parts(gate)
    hidden = (value * up).astype(jnp.bfloat16)
    hidden_grad = jnp.dot(cot_ref[...], weights[2], preferred_element_type=jnp.float32)
    gate_grad = (hidden_grad * up * slope).astype(jnp.bfloat16)
    up_grad = (hidden_grad * value).astype(jnp.bfloat16)
    acts[0] = gate_grad
    acts[1] = up_grad
    acts[2] = hidden
    keep_acts = pltpu.make_async_copy(acts, acts_ref.at[:, own_rows, :], ssem.at[2])
    keep_acts.start()

    def h_copy(j, d):
        at = acts_ref.at[:, pl.ds(pl.multiple_of(j * toks, 16), toks), :]
        return remote(acts, at, hsend.at[d], hrecv.at[j], {"wide": lax.rem(w + d, n_wide)})

    for d in range(1, n_wide):
        h_copy(w, d).start()

    def p_copy(t, src, to, d):
        return remote(
            parts.at[t, pl.ds(pl.multiple_of(to * piece, 16), piece), :], arrived.at[t, src],
            psend.at[t, d], precv.at[t, src], {"node": to},
        )

    out_part = contract_rows(hidden, weights[2])
    parts[0] = out_part.astype(jnp.bfloat16)
    for d in range(1, n_node):
        p_copy(0, n, lax.rem(n + d, n_node), d).start()
    parts[1] = (contract_rows(gate_grad, weights[0]) + contract_rows(up_grad, weights[1])).astype(jnp.bfloat16)
    for d in range(1, n_node):
        p_copy(1, n, lax.rem(n + d, n_node), d).start()

    def flip(b):
        bit = lax.rem(n // (1 << b), 2)
        return n + (1 - 2 * bit) * (1 << b)

    def held_at(b):
        base = n % (1 << (b + 1))
        return [base + i * (1 << (b + 1)) for i in range(n_node >> (b + 1))]

    def n_copy(j, q, b, slot):
        at = gath_ref.at[:, rows_of(j, q), :]
        return remote(at, at, nsend.at[j, slot], nrecv.at[j, q], {"node": flip(b)})

    def n_wait(j, q):
        n_copy(j, q, 0, 0).wait_recv()

    def hops(action, d):
        j = lax.rem(w + d, n_wide)
        slot = 0
        for b in reversed(range(bits)):
            for q in held_at(b):
                action(j, q, b, slot)
                slot += 1

    def first_hop(d):
        j = lax.rem(w + d, n_wide)
        x_copy(j, d, 0).wait_recv()
        x_copy(j, d, 1).wait_recv()
        n_copy(j, n, bits - 1, 0).start()

    out_refs = (mixed_ref, input_ref)

    def o_copy(t, src, to, d):
        at = out_refs[t].at[pl.ds(pl.multiple_of(src * piece, 16), piece), :]
        return remote(at, at, osend.at[t, d], orecv.at[t, src], {"node": to})

    def reduce_part(t):
        mine = pl.ds(pl.multiple_of(n * piece, 16), piece)
        acc = parts[t, mine, :].astype(jnp.float32)
        for d in range(1, n_node):
            src = lax.rem(n + d, n_node)
            p_copy(t, src, src, d).wait_recv()
            acc = acc + arrived[t, src].astype(jnp.float32)
        out_refs[t][mine, :] = acc.astype(jnp.bfloat16)
        for d in range(1, n_node):
            o_copy(t, n, lax.rem(n + d, n_node), d).start()

    for d in range(1, n_wide):
        first_hop(d)
    reduce_part(0)
    reduce_part(1)
    for d in range(1, n_wide):
        j = lax.rem(w + d, n_wide)
        slot = 1
        for b in reversed(range(bits - 1)):
            held = held_at(b)
            for q in held:
                @pl.when(lax.rem(q // (1 << (b + 1)), 2) != lax.rem(n // (1 << (b + 1)), 2))
                def _():
                    n_wait(j, q)
            for q in held:
                n_copy(j, q, b, slot).start()
                slot += 1
    last = [2 * i for i in range(n_node // 2)]
    for d in range(1, n_wide):
        j = lax.rem(w + d, n_wide)
        for i in last:
            n_wait(j, i + (1 - n % 2))
        h_copy(j, d).wait_recv()

    for t in range(2):
        for d in range(1, n_node):
            src = lax.rem(n + d, n_node)
            o_copy(t, src, src, d).wait_recv()
            o_copy(t, n, src, d).wait_send()
            p_copy(t, n, src, d).wait_send()
    for d in range(1, n_wide):
        x_copy(w, d, 0).wait_send()
        x_copy(w, d, 1).wait_send()
        h_copy(w, d).wait_send()
        hops(lambda j, q, b, slot: n_copy(j, q, b, slot).wait_send(), d)


    keep(0).wait()
    keep(1).wait()
    keep_acts.wait()


def main_call(inv, tokens, cotangent, blocks, n_wide, n_node):
    toks, width = tokens.shape
    dma = pltpu.SemaphoreType.DMA
    vmem = pl.BlockSpec(memory_space=pltpu.VMEM)
    smem = pl.BlockSpec(memory_space=pltpu.SMEM)
    hbm = pl.BlockSpec(memory_space=pl.ANY)
    bf16 = jnp.bfloat16
    return pl.pallas_call(
        functools.partial(main_kernel, n_wide, n_node),
        out_shape=(
            jax.ShapeDtypeStruct((toks, width), bf16),
            jax.ShapeDtypeStruct((toks, width), bf16),
            jax.ShapeDtypeStruct((2, n_wide * toks, width), bf16),
            jax.ShapeDtypeStruct((3, n_wide * toks, FF_DEV), bf16),
        ),
        in_specs=[smem, vmem, vmem, vmem],
        out_specs=(vmem, vmem, hbm, hbm),
        scratch_shapes=[
            pltpu.VMEM((3, width, FF_DEV), bf16),
            pltpu.VMEM((3, toks, FF_DEV), bf16),
            pltpu.VMEM((2, toks, width), bf16),
            pltpu.VMEM((2, n_node, toks // n_node, width), bf16),
            dma((n_wide, 2)), dma((n_wide, 2)), dma((n_wide, n_node)), dma((n_wide, n_node)),
            dma((n_wide,)), dma((n_wide,)), dma((2, n_node)), dma((2, n_node)), dma((2, n_node)), dma((2, n_node)),
            dma((3,)),
        ],
        compiler_params=pltpu.CompilerParams(
            collective_id=1, has_side_effects=True, vmem_limit_bytes=48 << 20
        ),
    )(inv, tokens, cotangent, blocks)


def grads_kernel(slots, rblocks, mine_ref, x_ref, acts_ref, out_ref, total):
    step = pl.program_id(0)
    per = rblocks * COLS

    @pl.when(step == 0)
    def _():
        total[...] = jnp.zeros_like(total)

    for s in range(slots):
        b = jnp.maximum(mine_ref[s], 0)
        m = b // per
        r = pl.multiple_of(((b // COLS) % rblocks) * EDGE, EDGE)
        c = pl.multiple_of((b % COLS) * EDGE, EDGE)
        total[s] += contract_tokens(x_ref[m // 2, :, pl.ds(r, EDGE)], acts_ref[m, :, pl.ds(c, EDGE)])

    @pl.when(step == pl.num_programs(0) - 1)
    def _():
        for s in range(slots):
            out_ref[s] = jnp.where(mine_ref[s] >= 0, total[s], 0.0).astype(out_ref.dtype)


def slot_grads(mine, gathered, acts, toks):
    slots = mine.shape[0]
    width = gathered.shape[2]
    return pl.pallas_call(
        functools.partial(grads_kernel, slots, width // EDGE),
        out_shape=jax.ShapeDtypeStruct((slots, EDGE, EDGE), jnp.bfloat16),
        grid_spec=pltpu.PrefetchScalarGridSpec(
            num_scalar_prefetch=1,
            grid=(gathered.shape[1] // toks,),
            in_specs=[
                pl.BlockSpec((2, toks, width), lambda j, ids: (0, j, 0)),
                pl.BlockSpec((3, toks, FF_DEV), lambda j, ids: (0, j, 0)),
            ],
            out_specs=pl.BlockSpec((slots, EDGE, EDGE), lambda j, ids: (0, 0, 0)),
            scratch_shapes=[pltpu.VMEM((slots, EDGE, EDGE), jnp.float32)],
        ),
        compiler_params=pltpu.CompilerParams(vmem_limit_bytes=24 << 20),
    )(mine, gathered, acts)


def per_device(n_wide, n_node, tokens, cotangent, tiles, tile_ids, tile_counts):
    slots = tiles.shape[2]
    ids = tile_ids.reshape(slots)
    mine = jnp.where(jnp.arange(slots, dtype=jnp.int32) < tile_counts[0, 0], ids, -1)
    padded = jnp.broadcast_to(jnp.pad(mine, (0, EDGE - slots), constant_values=-1)[None, :], (8, EDGE))
    gathered, all_ids = gather_tiles(tiles.reshape(slots * EDGE, EDGE), padded, n_wide)
    flat = all_ids[:, 0, :slots].reshape(1, n_wide * slots)
    numbers = jnp.arange(NBLK, dtype=jnp.int32)[:, None]
    none = n_wide * slots
    inv = jnp.min(jnp.where(flat == numbers, jnp.arange(none, dtype=jnp.int32)[None, :], none), axis=1)
    blocks = gathered.reshape(none + 1, EDGE, EDGE)
    mixed, input_grad, all_x, all_acts = main_call(inv, tokens, cotangent, blocks, n_wide, n_node)
    grads = slot_grads(mine, all_x, all_acts, tokens.shape[0])
    return mixed, input_grad, grads[None, None]


def solution(mesh):
    return jax.shard_map(
        functools.partial(per_device, mesh.shape["wide"], mesh.shape["node"]),
        mesh=mesh,
        in_specs=(
            P(("groups", "wide"), None),
            P(("groups", "wide"), None),
            P("node", "wide", None, None, None),
            P("node", "wide", None),
            P("node", "wide"),
        ),
        out_specs=(
            P(("groups", "wide"), None),
            P(("groups", "wide"), None),
            P(("groups", "node"), "wide", None, None, None),
        ),
        check_vma=False,
    )
```

```python
import functools
import math

import jax
import jax.numpy as jnp
from jax import lax
from jax.experimental import pallas as pl
from jax.experimental.pallas import tpu as pltpu
from jax.sharding import PartitionSpec as P

FF_DEV = 512
NBLK = 216
EDGE = 128
COLS = FF_DEV // EDGE
MESH = pl.DeviceIdType.MESH

gelu_scale = math.sqrt(2.0 / math.pi)
cubic_term = 0.044715


def gelu_parts(pre):
    tangent = jnp.tanh(gelu_scale * (pre + cubic_term * pre * pre * pre))
    value = 0.5 * pre * (1.0 + tangent)
    slope = 0.5 * (1.0 + tangent) + 0.5 * pre * (1.0 - tangent * tangent) * gelu_scale * (
        1.0 + 3.0 * cubic_term * pre * pre
    )
    return (value, slope)


def contract_rows(left, right):
    return lax.dot_general(
        left, right, (((1,), (1,)), ((), ())), preferred_element_type=jnp.float32
    )


def contract_tokens(left, right):
    return lax.dot_general(
        left, right, (((0,), (0,)), ((), ())), preferred_element_type=jnp.float32
    )


def remote(src, dst, send, recv, where):
    return pltpu.make_async_remote_copy(
        src_ref=src, dst_ref=dst, send_sem=send, recv_sem=recv, device_id=where, device_id_type=MESH
    )


def gather_kernel(n_wide, chunks, tiles_ref, ids_ref, all_ref, allids_ref,
                  zsend, zrecv, ysend, yrecv, isend, irecv, own_sem):
    w = lax.axis_index("wide")
    g = lax.axis_index("groups")
    other = 1 - g
    rows = tiles_ref.shape[0]
    half = rows // 2
    step = half // chunks

    barrier = pltpu.get_barrier_semaphore()
    for d in range(1, n_wide):
        pl.semaphore_signal(barrier, inc=1, device_id={"wide": lax.rem(w + d, n_wide)}, device_id_type=MESH)
    pl.semaphore_signal(barrier, inc=1, device_id={"groups": other}, device_id_type=MESH)
    own = pltpu.make_async_copy(tiles_ref, all_ref.at[pl.ds(pl.multiple_of(w * rows, 16), rows)], own_sem)
    own.start()
    all_ref[n_wide * rows:, :] = jnp.zeros((EDGE, EDGE), all_ref.dtype)
    allids_ref[w] = ids_ref[...]
    pl.semaphore_wait(barrier, n_wide)

    def part(group, k):
        return pl.ds(pl.multiple_of(group * half + k * step, 16), step)

    def piece(j, group, k):
        return all_ref.at[pl.ds(pl.multiple_of(j * rows + group * half + k * step, 16), step)]

    def z_copy(j, k, way):
        return remote(
            piece(j, g, k), piece(j, g, k),
            zsend.at[0 if way > 0 else 1, j, k], zrecv.at[j, k], {"wide": w + way},
        )

    def z_own(k, way):
        return remote(
            tiles_ref.at[part(g, k)], piece(w, g, k),
            zsend.at[0 if way > 0 else 1, w, k], zrecv.at[w, k], {"wide": w + way},
        )

    def y_copy(j, k, group):
        return remote(
            piece(j, group, k), piece(j, group, k),
            ysend.at[j, k], yrecv.at[j, k], {"groups": other},
        )

    def ids_copy(d):
        to = lax.rem(w + d, n_wide)
        return remote(allids_ref.at[w], allids_ref.at[w], isend.at[d], irecv.at[w], {"wide": to})

    right = w < n_wide - 1
    left = w > 0
    for k in range(chunks):
        @pl.when(right)
        def _():
            z_own(k, 1).start()

        @pl.when(left)
        def _():
            z_own(k, -1).start()
    for d in range(1, n_wide):
        ids_copy(d).start()
    for d in range(1, n_wide):
        for k in range(chunks):
            for way in (1, -1):
                j = w - d * way
                have = (j >= 0) if way > 0 else (j < n_wide)

                @pl.when(have)
                def _():
                    z_copy(j, k, way).wait_recv()

                @pl.when(have & (right if way > 0 else left))
                def _():
                    z_copy(j, k, way).start()

                @pl.when(have)
                def _():
                    y_copy(j, k, g).start()
    own.wait()
    for k in range(chunks):
        @pl.when(right)
        def _():
            z_own(k, 1).wait_send()

        @pl.when(left)
        def _():
            z_own(k, -1).wait_send()
    for d in range(1, n_wide):
        ids_copy(d).wait_send()
        j = lax.rem(w + d, n_wide)
        remote(allids_ref.at[j], allids_ref.at[j], isend.at[d], irecv.at[j], {"wide": j}).wait_recv()
        for k in range(chunks):
            y_copy(j, k, g).wait_send()
            y_copy(j, k, other).wait_recv()
            for way in (1, -1):
                i = w - d * way
                have = (i >= 0) if way > 0 else (i < n_wide)

                @pl.when(have & (right if way > 0 else left))
                def _():
                    z_copy(i, k, way).wait_send()


def gather_tiles(tiles, ids, n_wide):
    rows = tiles.shape[0]
    chunks = 5 if (rows // 2) % 80 == 0 else 1
    dma = pltpu.SemaphoreType.DMA
    vmem = pl.BlockSpec(memory_space=pltpu.VMEM)
    return pl.pallas_call(
        functools.partial(gather_kernel, n_wide, chunks),
        out_shape=(
            jax.ShapeDtypeStruct((n_wide * rows + EDGE, EDGE), tiles.dtype),
            jax.ShapeDtypeStruct((n_wide,) + ids.shape, ids.dtype),
        ),
        in_specs=[vmem, vmem],
        out_specs=(vmem, vmem),
        scratch_shapes=[
            dma((2, n_wide, chunks)), dma((n_wide, chunks)), dma((n_wide, chunks)), dma((n_wide, chunks)),
            dma((n_wide,)), dma((n_wide,)), dma,
        ],
        compiler_params=pltpu.CompilerParams(
            collective_id=0, has_side_effects=True, vmem_limit_bytes=40 << 20
        ),
    )(tiles, ids)


def main_kernel(n_wide, n_node,
                inv_ref, tok_ref, cot_ref, tiles_ref,
                mixed_ref, input_ref, gath_ref, acts_ref,
                weights, acts, parts, arrived,
                xsend, xrecv, nsend, nrecv, hsend, hrecv, psend, precv, osend, orecv, ssem):
    w = lax.axis_index("wide")
    n = lax.axis_index("node")
    toks, width = tok_ref.shape
    piece = toks // n_node
    rblocks = width // EDGE
    per = rblocks * COLS
    bits = n_node.bit_length() - 1

    barrier = pltpu.get_barrier_semaphore()
    for d in range(1, n_wide):
        pl.semaphore_signal(barrier, inc=1, device_id={"wide": lax.rem(w + d, n_wide)}, device_id_type=MESH)
    for d in range(1, n_node):
        pl.semaphore_signal(barrier, inc=1, device_id={"node": lax.rem(n + d, n_node)}, device_id_type=MESH)

    def rows_of(j, q):
        return pl.ds(pl.multiple_of(j * toks + q * piece, 16), piece)

    own_rows = pl.ds(pl.multiple_of(w * toks, 16), toks)
    def keep(t):
        return pltpu.make_async_copy((tok_ref, cot_ref)[t], gath_ref.at[t, own_rows, :], ssem.at[t])

    keep(0).start()
    keep(1).start()
    pl.semaphore_wait(barrier, n_wide + n_node - 2)

    def both_ways(d, action):
        for way in (1, -1):
            j = w - d * way
            have = (j >= 0) if way > 0 else (j < n_wide)
            more = (w < n_wide - 1) if way > 0 else (w > 0)
            action(j, way, have, more)

    def x_copy(j, way, t, own=False):
        to = gath_ref.at[t, rows_of(j, n), :]
        mine = (tok_ref, cot_ref)[t].at[pl.ds(pl.multiple_of(n * piece, 16), piece), :]
        return remote(
            mine if own else to, to, xsend.at[0 if way > 0 else 1, j, t], xrecv.at[j, t], {"wide": w + way}
        )

    def x_begin(j, way, have, more):
        @pl.when(more)
        def _():
            for t in range(2):
                x_copy(j, way, t, True).start()

    def x_pass(j, way, have, more):
        @pl.when(have)
        def _():
            for t in range(2):
                x_copy(j, way, t).wait_recv()

        @pl.when(have & more)
        def _():
            for t in range(2):
                x_copy(j, way, t).start()

        @pl.when(have)
        def _():
            n_copy(j, n, bits - 1, 0).start()

    def x_sent(j, way, have, more):
        @pl.when(have & more)
        def _():
            for t in range(2):
                x_copy(j, way, t).wait_send()

    def flip(b):
        bit = lax.rem(n // (1 << b), 2)
        return n + (1 - 2 * bit) * (1 << b)

    def held_at(b):
        base = n % (1 << (b + 1))
        return [base + i * (1 << (b + 1)) for i in range(n_node >> (b + 1))]

    def n_copy(j, q, b, slot):
        at = gath_ref.at[:, rows_of(j, q), :]
        return remote(at, at, nsend.at[j, slot], nrecv.at[j, q], {"node": flip(b)})

    def n_wait(j, q):
        n_copy(j, q, 0, 0).wait_recv()

    def hops(action, d):
        j = lax.rem(w + d, n_wide)
        slot = 0
        for b in reversed(range(bits)):
            for q in held_at(b):
                action(j, q, b, slot)
                slot += 1

    both_ways(0, x_begin)

    def place(r, _):
        for m in range(3):
            for c in range(COLS):
                i = inv_ref[m * per + r * COLS + c]
                weights[m, pl.ds(pl.multiple_of(r * EDGE, EDGE), EDGE), c * EDGE:(c + 1) * EDGE] = tiles_ref[i]
        return 0

    lax.fori_loop(0, rblocks, place, 0)

    gate = jnp.dot(tok_ref[...], weights[0], preferred_element_type=jnp.float32)
    up = jnp.dot(tok_ref[...], weights[1], preferred_element_type=jnp.float32)
    both_ways(1, x_pass)
    value, slope = gelu_parts(gate)
    hidden = (value * up).astype(jnp.bfloat16)
    hidden_grad = jnp.dot(cot_ref[...], weights[2], preferred_element_type=jnp.float32)
    gate_grad = (hidden_grad * up * slope).astype(jnp.bfloat16)
    up_grad = (hidden_grad * value).astype(jnp.bfloat16)
    acts[0] = gate_grad
    acts[1] = up_grad
    acts[2] = hidden
    keep_acts = pltpu.make_async_copy(acts, acts_ref.at[:, own_rows, :], ssem.at[2])
    keep_acts.start()

    def h_copy(j, way, own=False):
        at = acts_ref.at[:, pl.ds(pl.multiple_of(j * toks, 16), toks), :]
        return remote(
            acts if own else at, at, hsend.at[0 if way > 0 else 1, j], hrecv.at[j], {"wide": w + way}
        )

    def h_begin(j, way, have, more):
        @pl.when(more)
        def _():
            h_copy(j, way, True).start()

    def h_pass(j, way, have, more):
        @pl.when(have)
        def _():
            h_copy(j, way).wait_recv()

        @pl.when(have & more)
        def _():
            h_copy(j, way).start()

    def h_sent(j, way, have, more):
        @pl.when(have & more)
        def _():
            h_copy(j, way).wait_send()

    both_ways(0, h_begin)

    def p_copy(t, src, to, d):
        return remote(
            parts.at[t, pl.ds(pl.multiple_of(to * piece, 16), piece), :], arrived.at[t, src],
            psend.at[t, d], precv.at[t, src], {"node": to},
        )

    out_part = contract_rows(hidden, weights[2])
    parts[0] = out_part.astype(jnp.bfloat16)
    for d in range(1, n_node):
        p_copy(0, n, lax.rem(n + d, n_node), d).start()
    if n_wide > 2:
        both_ways(2, x_pass)
    parts[1] = (contract_rows(gate_grad, weights[0]) + contract_rows(up_grad, weights[1])).astype(jnp.bfloat16)
    for d in range(1, n_node):
        p_copy(1, n, lax.rem(n + d, n_node), d).start()

    out_refs = (mixed_ref, input_ref)

    def o_copy(t, src, to, d):
        at = out_refs[t].at[pl.ds(pl.multiple_of(src * piece, 16), piece), :]
        return remote(at, at, osend.at[t, d], orecv.at[t, src], {"node": to})

    def reduce_part(t):
        mine = pl.ds(pl.multiple_of(n * piece, 16), piece)
        acc = parts[t, mine, :].astype(jnp.float32)
        for d in range(1, n_node):
            src = lax.rem(n + d, n_node)
            p_copy(t, src, src, d).wait_recv()
            acc = acc + arrived[t, src].astype(jnp.float32)
        out_refs[t][mine, :] = acc.astype(jnp.bfloat16)
        for d in range(1, n_node):
            o_copy(t, n, lax.rem(n + d, n_node), d).start()

    both_ways(1, h_pass)
    reduce_part(0)
    for d in range(3, n_wide):
        both_ways(d, x_pass)
        both_ways(d - 1, h_pass)
    reduce_part(1)
    for d in range(1, n_wide):
        j = lax.rem(w + d, n_wide)
        slot = 1
        for b in reversed(range(bits - 1)):
            held = held_at(b)
            for q in held:
                @pl.when(lax.rem(q // (1 << (b + 1)), 2) != lax.rem(n // (1 << (b + 1)), 2))
                def _():
                    n_wait(j, q)
            for q in held:
                n_copy(j, q, b, slot).start()
                slot += 1
    last = [2 * i for i in range(n_node // 2)]
    for d in range(1, n_wide):
        j = lax.rem(w + d, n_wide)
        for i in last:
            n_wait(j, i + (1 - n % 2))
    both_ways(n_wide - 1, h_pass)

    for t in range(2):
        for d in range(1, n_node):
            src = lax.rem(n + d, n_node)
            o_copy(t, src, src, d).wait_recv()
            o_copy(t, n, src, d).wait_send()
            p_copy(t, n, src, d).wait_send()
    for d in range(1, n_wide):
        hops(lambda j, q, b, slot: n_copy(j, q, b, slot).wait_send(), d)


    for d in range(n_wide):
        both_ways(d, x_sent)
        both_ways(d, h_sent)
    keep(0).wait()
    keep(1).wait()
    keep_acts.wait()


def main_call(inv, tokens, cotangent, blocks, n_wide, n_node):
    toks, width = tokens.shape
    dma = pltpu.SemaphoreType.DMA
    vmem = pl.BlockSpec(memory_space=pltpu.VMEM)
    smem = pl.BlockSpec(memory_space=pltpu.SMEM)
    hbm = pl.BlockSpec(memory_space=pl.ANY)
    bf16 = jnp.bfloat16
    return pl.pallas_call(
        functools.partial(main_kernel, n_wide, n_node),
        out_shape=(
            jax.ShapeDtypeStruct((toks, width), bf16),
            jax.ShapeDtypeStruct((toks, width), bf16),
            jax.ShapeDtypeStruct((2, n_wide * toks, width), bf16),
            jax.ShapeDtypeStruct((3, n_wide * toks, FF_DEV), bf16),
        ),
        in_specs=[smem, vmem, vmem, vmem],
        out_specs=(vmem, vmem, hbm, hbm),
        scratch_shapes=[
            pltpu.VMEM((3, width, FF_DEV), bf16),
            pltpu.VMEM((3, toks, FF_DEV), bf16),
            pltpu.VMEM((2, toks, width), bf16),
            pltpu.VMEM((2, n_node, toks // n_node, width), bf16),
            dma((2, n_wide, 2)), dma((n_wide, 2)), dma((n_wide, n_node)), dma((n_wide, n_node)),
            dma((2, n_wide)), dma((n_wide,)), dma((2, n_node)), dma((2, n_node)), dma((2, n_node)), dma((2, n_node)),
            dma((3,)),
        ],
        compiler_params=pltpu.CompilerParams(
            collective_id=1, has_side_effects=True, vmem_limit_bytes=48 << 20
        ),
    )(inv, tokens, cotangent, blocks)


def grads_kernel(slots, rblocks, mine_ref, x_ref, acts_ref, out_ref, total):
    step = pl.program_id(0)
    per = rblocks * COLS

    @pl.when(step == 0)
    def _():
        total[...] = jnp.zeros_like(total)

    for s in range(slots):
        b = jnp.maximum(mine_ref[s], 0)
        m = b // per
        r = pl.multiple_of(((b // COLS) % rblocks) * EDGE, EDGE)
        c = pl.multiple_of((b % COLS) * EDGE, EDGE)
        total[s] += contract_tokens(x_ref[m // 2, :, pl.ds(r, EDGE)], acts_ref[m, :, pl.ds(c, EDGE)])

    @pl.when(step == pl.num_programs(0) - 1)
    def _():
        for s in range(slots):
            out_ref[s] = jnp.where(mine_ref[s] >= 0, total[s], 0.0).astype(out_ref.dtype)


def slot_grads(mine, gathered, acts, toks):
    slots = mine.shape[0]
    width = gathered.shape[2]
    return pl.pallas_call(
        functools.partial(grads_kernel, slots, width // EDGE),
        out_shape=jax.ShapeDtypeStruct((slots, EDGE, EDGE), jnp.bfloat16),
        grid_spec=pltpu.PrefetchScalarGridSpec(
            num_scalar_prefetch=1,
            grid=(gathered.shape[1] // toks,),
            in_specs=[
                pl.BlockSpec((2, toks, width), lambda j, ids: (0, j, 0)),
                pl.BlockSpec((3, toks, FF_DEV), lambda j, ids: (0, j, 0)),
            ],
            out_specs=pl.BlockSpec((slots, EDGE, EDGE), lambda j, ids: (0, 0, 0)),
            scratch_shapes=[pltpu.VMEM((slots, EDGE, EDGE), jnp.float32)],
        ),
        compiler_params=pltpu.CompilerParams(vmem_limit_bytes=24 << 20),
    )(mine, gathered, acts)


def per_device(n_wide, n_node, tokens, cotangent, tiles, tile_ids, tile_counts):
    slots = tiles.shape[2]
    ids = tile_ids.reshape(slots)
    mine = jnp.where(jnp.arange(slots, dtype=jnp.int32) < tile_counts[0, 0], ids, -1)
    padded = jnp.broadcast_to(jnp.pad(mine, (0, EDGE - slots), constant_values=-1)[None, :], (8, EDGE))
    gathered, all_ids = gather_tiles(tiles.reshape(slots * EDGE, EDGE), padded, n_wide)
    flat = all_ids[:, 0, :slots].reshape(1, n_wide * slots)
    numbers = jnp.arange(NBLK, dtype=jnp.int32)[:, None]
    none = n_wide * slots
    inv = jnp.min(jnp.where(flat == numbers, jnp.arange(none, dtype=jnp.int32)[None, :], none), axis=1)
    blocks = gathered.reshape(none + 1, EDGE, EDGE)
    mixed, input_grad, all_x, all_acts = main_call(inv, tokens, cotangent, blocks, n_wide, n_node)
    grads = slot_grads(mine, all_x, all_acts, tokens.shape[0])
    return mixed, input_grad, grads[None, None]


def solution(mesh):
    return jax.shard_map(
        functools.partial(per_device, mesh.shape["wide"], mesh.shape["node"]),
        mesh=mesh,
        in_specs=(
            P(("groups", "wide"), None),
            P(("groups", "wide"), None),
            P("node", "wide", None, None, None),
            P("node", "wide", None),
            P("node", "wide"),
        ),
        out_specs=(
            P(("groups", "wide"), None),
            P(("groups", "wide"), None),
            P(("groups", "node"), "wide", None, None, None),
        ),
        check_vma=False,
    )
```

```python
import functools
import math

import jax
import jax.numpy as jnp
from jax import lax
from jax.experimental import pallas as pl
from jax.experimental.pallas import tpu as pltpu
from jax.sharding import PartitionSpec as P

FF_DEV = 512
EDGE = 128
COLS = FF_DEV // EDGE
MESH = pl.DeviceIdType.MESH

gelu_scale = math.sqrt(2.0 / math.pi)
cubic_term = 0.044715


def gelu_parts(pre):
    tangent = jnp.tanh(gelu_scale * (pre + cubic_term * pre * pre * pre))
    value = 0.5 * pre * (1.0 + tangent)
    slope = 0.5 * (1.0 + tangent) + 0.5 * pre * (1.0 - tangent * tangent) * gelu_scale * (
        1.0 + 3.0 * cubic_term * pre * pre
    )
    return (value, slope)


def contract_rows(left, right):
    return lax.dot_general(
        left, right, (((1,), (1,)), ((), ())), preferred_element_type=jnp.float32
    )


def contract_tokens(left, right):
    return lax.dot_general(
        left, right, (((0,), (0,)), ((), ())), preferred_element_type=jnp.float32
    )


def remote(src, dst, send, recv, where):
    return pltpu.make_async_remote_copy(
        src_ref=src, dst_ref=dst, send_sem=send, recv_sem=recv, device_id=where, device_id_type=MESH
    )


def main_kernel(n_wide, n_node, chunks,
                ids_ref, tok_ref, cot_ref, tiles_ref,
                mixed_ref, input_ref, gath_ref, acts_ref,
                blocks, all_ids, ids_now, inv_vec, inv_ref, weights, acts, parts, arrived,
                zsend, zrecv, ysend, yrecv, isend, irecv, lsem,
                xsend, xrecv, nsend, nrecv, hsend, hrecv, psend, precv, osend, orecv, ssem):
    w = lax.axis_index("wide")
    n = lax.axis_index("node")
    g = lax.axis_index("groups")
    other = 1 - g
    slots = tiles_ref.shape[0]
    step = slots // chunks
    none = n_wide * slots
    toks, width = tok_ref.shape
    piece = toks // n_node
    rblocks = width // EDGE
    per = rblocks * COLS
    bits = n_node.bit_length() - 1

    barrier = pltpu.get_barrier_semaphore()
    for d in range(1, n_wide):
        pl.semaphore_signal(barrier, inc=1, device_id={"wide": lax.rem(w + d, n_wide)}, device_id_type=MESH)
    for d in range(1, n_node):
        pl.semaphore_signal(barrier, inc=1, device_id={"node": lax.rem(n + d, n_node)}, device_id_type=MESH)

    pl.semaphore_signal(barrier, inc=1, device_id={"groups": other}, device_id_type=MESH)
    own_tiles = pltpu.make_async_copy(tiles_ref, blocks.at[pl.ds(w * slots, slots)], lsem.at[0])
    own_tiles.start()
    blocks[none] = jnp.zeros((EDGE, EDGE), blocks.dtype)
    all_ids[w] = ids_ref[...]

    def rows_of(j, q):
        return pl.ds(pl.multiple_of(j * toks + q * piece, 16), piece)

    own_rows = pl.ds(pl.multiple_of(w * toks, 16), toks)
    def keep(t):
        return pltpu.make_async_copy((tok_ref, cot_ref)[t], gath_ref.at[t, own_rows, :], ssem.at[t])

    keep(0).start()
    keep(1).start()
    pl.semaphore_wait(barrier, n_wide + n_node - 1)

    def both_ways(d, action):
        for way in (1, -1):
            j = w - d * way
            have = (j >= 0) if way > 0 else (j < n_wide)
            more = (w < n_wide - 1) if way > 0 else (w > 0)
            action(j, way, have, more)

    half = EDGE // 2

    def piece_of(j, group, k):
        return blocks.at[pl.ds(j * slots + k * step, step), pl.ds(pl.multiple_of(group * half, half), half), :]

    def z_copy(j, k, way, own=False):
        mine = tiles_ref.at[pl.ds(k * step, step), pl.ds(pl.multiple_of(g * half, half), half), :]
        to = piece_of(j, g, k)
        return remote(
            mine if own else to, to, zsend.at[0 if way > 0 else 1, j, k], zrecv.at[j, k], {"wide": w + way}
        )

    def y_copy(j, k, group):
        at = piece_of(j, group, k)
        return remote(at, at, ysend.at[j, k], yrecv.at[j, k], {"groups": other})

    def ids_copy(j, d, to):
        return remote(all_ids.at[j], all_ids.at[j], isend.at[d], irecv.at[j], {"wide": to})

    def z_pass(k):
        def go(j, way, have, more):
            @pl.when(have)
            def _():
                z_copy(j, k, way).wait_recv()

            @pl.when(have & more)
            def _():
                z_copy(j, k, way).start()

            @pl.when(have)
            def _():
                y_copy(j, k, g).start()
        return go

    def z_sent(j, way, have, more):
        @pl.when(have & more)
        def _():
            for k in range(chunks):
                z_copy(j, k, way).wait_send()

    def z_begin(k):
        def go(j, way, have, more):
            @pl.when(more)
            def _():
                z_copy(j, k, way, True).start()
        return go

    def x_copy(j, way, t, own=False):
        to = gath_ref.at[t, rows_of(j, n), :]
        mine = (tok_ref, cot_ref)[t].at[pl.ds(pl.multiple_of(n * piece, 16), piece), :]
        return remote(
            mine if own else to, to, xsend.at[0 if way > 0 else 1, j, t], xrecv.at[j, t], {"wide": w + way}
        )

    def x_begin(j, way, have, more):
        @pl.when(more)
        def _():
            for t in range(2):
                x_copy(j, way, t, True).start()

    def x_pass(j, way, have, more):
        @pl.when(have)
        def _():
            for t in range(2):
                x_copy(j, way, t).wait_recv()

        @pl.when(have & more)
        def _():
            for t in range(2):
                x_copy(j, way, t).start()

        @pl.when(have)
        def _():
            n_copy(j, n, bits - 1, 0).start()

    def x_sent(j, way, have, more):
        @pl.when(have & more)
        def _():
            for t in range(2):
                x_copy(j, way, t).wait_send()

    def flip(b):
        bit = lax.rem(n // (1 << b), 2)
        return n + (1 - 2 * bit) * (1 << b)

    def held_at(b):
        base = n % (1 << (b + 1))
        return [base + i * (1 << (b + 1)) for i in range(n_node >> (b + 1))]

    def n_copy(j, q, b, slot):
        at = gath_ref.at[:, rows_of(j, q), :]
        return remote(at, at, nsend.at[j, slot], nrecv.at[j, q], {"node": flip(b)})

    def n_wait(j, q):
        n_copy(j, q, 0, 0).wait_recv()

    def hops(action, d):
        j = lax.rem(w + d, n_wide)
        slot = 0
        for b in reversed(range(bits)):
            for q in held_at(b):
                action(j, q, b, slot)
                slot += 1

    for k in range(chunks):
        both_ways(0, z_begin(k))
    for d in range(1, n_wide):
        ids_copy(w, d, lax.rem(w + d, n_wide)).start()
    for d in range(1, n_wide - 1):
        for k in range(chunks):
            both_ways(d, z_pass(k))
    both_ways(0, x_begin)

    for d in range(1, n_wide):
        j = lax.rem(w + d, n_wide)
        ids_copy(j, d, j).wait_recv()
    ids_in = pltpu.make_async_copy(all_ids, ids_now, lsem.at[1])
    ids_in.start()
    ids_in.wait()
    number = lax.broadcasted_iota(jnp.int32, (8, EDGE), 0) * EDGE + lax.broadcasted_iota(jnp.int32, (8, EDGE), 1)

    def add_ids(j, found):
        for s in range(slots):
            hit = jnp.maximum(1 - jnp.abs(number - ids_now[j, 0, s]), 0)
            found = jnp.minimum(found, none + hit * (j * slots + s - none))
        return found

    inv_vec[...] = lax.fori_loop(0, n_wide, add_ids, jnp.full((8, EDGE), none, jnp.int32))
    inv_in = pltpu.make_async_copy(inv_vec, inv_ref, lsem.at[2])
    inv_in.start()
    inv_in.wait()

    for k in range(chunks):
        both_ways(n_wide - 1, z_pass(k))
    for d in range(1, n_wide):
        for k in range(chunks):
            y_copy(lax.rem(w + d, n_wide), k, other).wait_recv()
    own_tiles.wait()

    def place(r, _):
        for m in range(3):
            for c in range(COLS):
                b = m * per + r * COLS + c
                i = inv_ref[b // EDGE, b % EDGE]
                weights[m, pl.ds(pl.multiple_of(r * EDGE, EDGE), EDGE), c * EDGE:(c + 1) * EDGE] = blocks[i]
        return 0

    lax.fori_loop(0, rblocks, place, 0)
    both_ways(1, x_pass)

    gate = jnp.dot(tok_ref[...], weights[0], preferred_element_type=jnp.float32)
    up = jnp.dot(tok_ref[...], weights[1], preferred_element_type=jnp.float32)
    value, slope = gelu_parts(gate)
    hidden = (value * up).astype(jnp.bfloat16)
    hidden_grad = jnp.dot(cot_ref[...], weights[2], preferred_element_type=jnp.float32)
    gate_grad = (hidden_grad * up * slope).astype(jnp.bfloat16)
    up_grad = (hidden_grad * value).astype(jnp.bfloat16)
    acts[0] = gate_grad
    acts[1] = up_grad
    acts[2] = hidden
    keep_acts = pltpu.make_async_copy(acts, acts_ref.at[:, own_rows, :], ssem.at[2])
    keep_acts.start()

    def h_copy(j, way, own=False):
        at = acts_ref.at[:, pl.ds(pl.multiple_of(j * toks, 16), toks), :]
        return remote(
            acts if own else at, at, hsend.at[0 if way > 0 else 1, j], hrecv.at[j], {"wide": w + way}
        )

    def h_begin(j, way, have, more):
        @pl.when(more)
        def _():
            h_copy(j, way, True).start()

    def h_pass(j, way, have, more):
        @pl.when(have)
        def _():
            h_copy(j, way).wait_recv()

        @pl.when(have & more)
        def _():
            h_copy(j, way).start()

    def h_sent(j, way, have, more):
        @pl.when(have & more)
        def _():
            h_copy(j, way).wait_send()

    both_ways(0, h_begin)

    def p_copy(t, src, to, d):
        return remote(
            parts.at[t, pl.ds(pl.multiple_of(to * piece, 16), piece), :], arrived.at[t, src],
            psend.at[t, d], precv.at[t, src], {"node": to},
        )

    out_part = contract_rows(hidden, weights[2])
    parts[0] = out_part.astype(jnp.bfloat16)
    for d in range(1, n_node):
        p_copy(0, n, lax.rem(n + d, n_node), d).start()
    if n_wide > 2:
        both_ways(2, x_pass)
    parts[1] = (contract_rows(gate_grad, weights[0]) + contract_rows(up_grad, weights[1])).astype(jnp.bfloat16)
    for d in range(1, n_node):
        p_copy(1, n, lax.rem(n + d, n_node), d).start()

    out_refs = (mixed_ref, input_ref)

    def o_copy(t, src, to, d):
        at = out_refs[t].at[pl.ds(pl.multiple_of(src * piece, 16), piece), :]
        return remote(at, at, osend.at[t, d], orecv.at[t, src], {"node": to})

    def reduce_part(t):
        mine = pl.ds(pl.multiple_of(n * piece, 16), piece)
        acc = parts[t, mine, :].astype(jnp.float32)
        for d in range(1, n_node):
            src = lax.rem(n + d, n_node)
            p_copy(t, src, src, d).wait_recv()
            acc = acc + arrived[t, src].astype(jnp.float32)
        out_refs[t][mine, :] = acc.astype(jnp.bfloat16)
        for d in range(1, n_node):
            o_copy(t, n, lax.rem(n + d, n_node), d).start()

    both_ways(1, h_pass)
    reduce_part(0)
    for d in range(3, n_wide):
        both_ways(d, x_pass)
        both_ways(d - 1, h_pass)
    reduce_part(1)
    for d in range(1, n_wide):
        j = lax.rem(w + d, n_wide)
        slot = 1
        for b in reversed(range(bits - 1)):
            held = held_at(b)
            for q in held:
                @pl.when(lax.rem(q // (1 << (b + 1)), 2) != lax.rem(n // (1 << (b + 1)), 2))
                def _():
                    n_wait(j, q)
            for q in held:
                n_copy(j, q, b, slot).start()
                slot += 1
    last = [2 * i for i in range(n_node // 2)]
    for d in range(1, n_wide):
        j = lax.rem(w + d, n_wide)
        for i in last:
            n_wait(j, i + (1 - n % 2))
    both_ways(n_wide - 1, h_pass)

    for t in range(2):
        for d in range(1, n_node):
            src = lax.rem(n + d, n_node)
            o_copy(t, src, src, d).wait_recv()
            o_copy(t, n, src, d).wait_send()
            p_copy(t, n, src, d).wait_send()
    for d in range(1, n_wide):
        hops(lambda j, q, b, slot: n_copy(j, q, b, slot).wait_send(), d)


    for d in range(n_wide):
        both_ways(d, x_sent)
        both_ways(d, h_sent)
        both_ways(d, z_sent)
    for d in range(1, n_wide):
        j = lax.rem(w + d, n_wide)
        ids_copy(w, d, j).wait_send()
        for k in range(chunks):
            y_copy(j, k, g).wait_send()
    keep(0).wait()
    keep(1).wait()
    keep_acts.wait()


def main_call(ids, tokens, cotangent, tiles, n_wide, n_node):
    toks, width = tokens.shape
    dma = pltpu.SemaphoreType.DMA
    vmem = pl.BlockSpec(memory_space=pltpu.VMEM)
    slots = tiles.shape[0]
    chunks = 5 if slots % 5 == 0 else 1
    hbm = pl.BlockSpec(memory_space=pl.ANY)
    bf16 = jnp.bfloat16
    return pl.pallas_call(
        functools.partial(main_kernel, n_wide, n_node, chunks),
        out_shape=(
            jax.ShapeDtypeStruct((toks, width), bf16),
            jax.ShapeDtypeStruct((toks, width), bf16),
            jax.ShapeDtypeStruct((2, n_wide * toks, width), bf16),
            jax.ShapeDtypeStruct((3, n_wide * toks, FF_DEV), bf16),
        ),
        in_specs=[vmem, vmem, vmem, vmem],
        out_specs=(vmem, vmem, hbm, hbm),
        scratch_shapes=[
            pltpu.VMEM((n_wide * slots + 1, EDGE, EDGE), bf16),
            pltpu.VMEM((n_wide, 8, EDGE), jnp.int32),
            pltpu.SMEM((n_wide, 8, EDGE), jnp.int32),
            pltpu.VMEM((8, EDGE), jnp.int32),
            pltpu.SMEM((8, EDGE), jnp.int32),
            pltpu.VMEM((3, width, FF_DEV), bf16),
            pltpu.VMEM((3, toks, FF_DEV), bf16),
            pltpu.VMEM((2, toks, width), bf16),
            pltpu.VMEM((2, n_node, toks // n_node, width), bf16),
            dma((2, n_wide, chunks)), dma((n_wide, chunks)), dma((n_wide, chunks)), dma((n_wide, chunks)),
            dma((n_wide,)), dma((n_wide,)), dma((3,)),
            dma((2, n_wide, 2)), dma((n_wide, 2)), dma((n_wide, n_node)), dma((n_wide, n_node)),
            dma((2, n_wide)), dma((n_wide,)), dma((2, n_node)), dma((2, n_node)), dma((2, n_node)), dma((2, n_node)),
            dma((3,)),
        ],
        compiler_params=pltpu.CompilerParams(
            collective_id=1, has_side_effects=True, vmem_limit_bytes=48 << 20
        ),
    )(ids, tokens, cotangent, tiles)


def grads_kernel(slots, rblocks, mine_ref, x_ref, acts_ref, out_ref, total):
    step = pl.program_id(0)
    per = rblocks * COLS

    @pl.when(step == 0)
    def _():
        total[...] = jnp.zeros_like(total)

    for s in range(slots):
        b = jnp.maximum(mine_ref[s], 0)
        m = b // per
        r = pl.multiple_of(((b // COLS) % rblocks) * EDGE, EDGE)
        c = pl.multiple_of((b % COLS) * EDGE, EDGE)
        total[s] += contract_tokens(x_ref[m // 2, :, pl.ds(r, EDGE)], acts_ref[m, :, pl.ds(c, EDGE)])

    @pl.when(step == pl.num_programs(0) - 1)
    def _():
        for s in range(slots):
            out_ref[s] = jnp.where(mine_ref[s] >= 0, total[s], 0.0).astype(out_ref.dtype)


def slot_grads(mine, gathered, acts, toks):
    slots = mine.shape[0]
    width = gathered.shape[2]
    return pl.pallas_call(
        functools.partial(grads_kernel, slots, width // EDGE),
        out_shape=jax.ShapeDtypeStruct((slots, EDGE, EDGE), jnp.bfloat16),
        grid_spec=pltpu.PrefetchScalarGridSpec(
            num_scalar_prefetch=1,
            grid=(gathered.shape[1] // toks,),
            in_specs=[
                pl.BlockSpec((2, toks, width), lambda j, ids: (0, j, 0)),
                pl.BlockSpec((3, toks, FF_DEV), lambda j, ids: (0, j, 0)),
            ],
            out_specs=pl.BlockSpec((slots, EDGE, EDGE), lambda j, ids: (0, 0, 0)),
            scratch_shapes=[pltpu.VMEM((slots, EDGE, EDGE), jnp.float32)],
        ),
        compiler_params=pltpu.CompilerParams(vmem_limit_bytes=24 << 20),
    )(mine, gathered, acts)


def per_device(n_wide, n_node, tokens, cotangent, tiles, tile_ids, tile_counts):
    slots = tiles.shape[2]
    ids = tile_ids.reshape(slots)
    mine = jnp.where(jnp.arange(slots, dtype=jnp.int32) < tile_counts[0, 0], ids, -1)
    padded = jnp.broadcast_to(jnp.pad(mine, (0, EDGE - slots), constant_values=-1)[None, :], (8, EDGE))
    mixed, input_grad, all_x, all_acts = main_call(
        padded, tokens, cotangent, tiles.reshape(slots, EDGE, EDGE), n_wide, n_node
    )
    grads = slot_grads(mine, all_x, all_acts, tokens.shape[0])
    return mixed, input_grad, grads[None, None]


def solution(mesh):
    return jax.shard_map(
        functools.partial(per_device, mesh.shape["wide"], mesh.shape["node"]),
        mesh=mesh,
        in_specs=(
            P(("groups", "wide"), None),
            P(("groups", "wide"), None),
            P("node", "wide", None, None, None),
            P("node", "wide", None),
            P("node", "wide"),
        ),
        out_specs=(
            P(("groups", "wide"), None),
            P(("groups", "wide"), None),
            P(("groups", "node"), "wide", None, None, None),
        ),
        check_vma=False,
    )
```

```python
import functools
import math

import jax
import jax.numpy as jnp
from jax import lax
from jax.experimental import pallas as pl
from jax.experimental.pallas import tpu as pltpu
from jax.sharding import PartitionSpec as P

FF_DEV = 512
EDGE = 128
COLS = FF_DEV // EDGE
MESH = pl.DeviceIdType.MESH

gelu_scale = math.sqrt(2.0 / math.pi)
cubic_term = 0.044715


def gelu_parts(pre):
    tangent = jnp.tanh(gelu_scale * (pre + cubic_term * pre * pre * pre))
    value = 0.5 * pre * (1.0 + tangent)
    slope = 0.5 * (1.0 + tangent) + 0.5 * pre * (1.0 - tangent * tangent) * gelu_scale * (
        1.0 + 3.0 * cubic_term * pre * pre
    )
    return (value, slope)


def contract_rows(left, right):
    return lax.dot_general(
        left, right, (((1,), (1,)), ((), ())), preferred_element_type=jnp.float32
    )


def contract_tokens(left, right):
    return lax.dot_general(
        left, right, (((0,), (0,)), ((), ())), preferred_element_type=jnp.float32
    )


def remote(src, dst, send, recv, where):
    return pltpu.make_async_remote_copy(
        src_ref=src, dst_ref=dst, send_sem=send, recv_sem=recv, device_id=where, device_id_type=MESH
    )


def main_kernel(n_wide, n_node, chunks,
                ids_ref, tok_ref, cot_ref, tiles_ref,
                mixed_ref, input_ref, gath_ref, acts_ref,
                blocks, all_ids, ids_now, inv_vec, inv_ref, tok_now, cot_now, weights, acts, parts, arrived,
                zsend, zrecv, ysend, yrecv, isend, irecv, lsem,
                xsend, xrecv, nsend, nrecv, hsend, hrecv, psend, precv, osend, orecv, ssem):
    w = lax.axis_index("wide")
    n = lax.axis_index("node")
    g = lax.axis_index("groups")
    other = 1 - g
    slots = tiles_ref.shape[0]
    step = slots // chunks
    none = n_wide * slots
    toks, width = tok_ref.shape
    piece = toks // n_node
    rblocks = width // EDGE
    per = rblocks * COLS
    bits = n_node.bit_length() - 1

    barrier = pltpu.get_barrier_semaphore()
    for d in range(1, n_wide):
        pl.semaphore_signal(barrier, inc=1, device_id={"wide": lax.rem(w + d, n_wide)}, device_id_type=MESH)
    for d in range(1, n_node):
        pl.semaphore_signal(barrier, inc=1, device_id={"node": lax.rem(n + d, n_node)}, device_id_type=MESH)

    pl.semaphore_signal(barrier, inc=1, device_id={"groups": other}, device_id_type=MESH)
    own_tiles = pltpu.make_async_copy(tiles_ref, blocks.at[pl.ds(w * slots, slots)], lsem.at[0])
    own_tiles.start()
    blocks[none] = jnp.zeros((EDGE, EDGE), blocks.dtype)
    all_ids[w] = ids_ref[...]

    def rows_of(j, q):
        return pl.ds(pl.multiple_of(j * toks + q * piece, 16), piece)

    own_rows = pl.ds(pl.multiple_of(w * toks, 16), toks)
    def keep(t):
        return pltpu.make_async_copy((tok_ref, cot_ref)[t], gath_ref.at[t, own_rows, :], ssem.at[t])

    def load(t):
        return pltpu.make_async_copy((tok_ref, cot_ref)[t], (tok_now, cot_now)[t], lsem.at[3 + t])

    pl.semaphore_wait(barrier, n_wide + n_node - 1)

    def both_ways(d, action):
        for way in (1, -1):
            j = w - d * way
            have = (j >= 0) if way > 0 else (j < n_wide)
            more = (w < n_wide - 1) if way > 0 else (w > 0)
            action(j, way, have, more)

    half = EDGE // 2

    def piece_of(j, group, k):
        return blocks.at[pl.ds(j * slots + k * step, step), pl.ds(pl.multiple_of(group * half, half), half), :]

    def z_copy(j, k, way, own=False):
        mine = tiles_ref.at[pl.ds(k * step, step), pl.ds(pl.multiple_of(g * half, half), half), :]
        to = piece_of(j, g, k)
        return remote(
            mine if own else to, to, zsend.at[0 if way > 0 else 1, j, k], zrecv.at[j, k], {"wide": w + way}
        )

    def y_copy(j, k, group):
        at = piece_of(j, group, k)
        return remote(at, at, ysend.at[j, k], yrecv.at[j, k], {"groups": other})

    def ids_copy(j, d, to):
        return remote(all_ids.at[j], all_ids.at[j], isend.at[d], irecv.at[j], {"wide": to})

    def z_pass(k):
        def go(j, way, have, more):
            @pl.when(have)
            def _():
                z_copy(j, k, way).wait_recv()

            @pl.when(have & more)
            def _():
                z_copy(j, k, way).start()

            @pl.when(have)
            def _():
                y_copy(j, k, g).start()
        return go

    def z_sent(j, way, have, more):
        @pl.when(have & more)
        def _():
            for k in range(chunks):
                z_copy(j, k, way).wait_send()

    def z_begin(k):
        def go(j, way, have, more):
            @pl.when(more)
            def _():
                z_copy(j, k, way, True).start()
        return go

    def x_copy(j, way, t, own=False):
        to = gath_ref.at[t, rows_of(j, n), :]
        mine = (tok_ref, cot_ref)[t].at[pl.ds(pl.multiple_of(n * piece, 16), piece), :]
        return remote(
            mine if own else to, to, xsend.at[0 if way > 0 else 1, j, t], xrecv.at[j, t], {"wide": w + way}
        )

    def x_begin(j, way, have, more):
        @pl.when(more)
        def _():
            for t in range(2):
                x_copy(j, way, t, True).start()

    def x_pass(j, way, have, more):
        @pl.when(have)
        def _():
            for t in range(2):
                x_copy(j, way, t).wait_recv()

        @pl.when(have & more)
        def _():
            for t in range(2):
                x_copy(j, way, t).start()

        @pl.when(have)
        def _():
            n_copy(j, n, bits - 1, 0).start()

    def x_sent(j, way, have, more):
        @pl.when(have & more)
        def _():
            for t in range(2):
                x_copy(j, way, t).wait_send()

    def flip(b):
        bit = lax.rem(n // (1 << b), 2)
        return n + (1 - 2 * bit) * (1 << b)

    def held_at(b):
        base = n % (1 << (b + 1))
        return [base + i * (1 << (b + 1)) for i in range(n_node >> (b + 1))]

    def n_copy(j, q, b, slot):
        at = gath_ref.at[:, rows_of(j, q), :]
        return remote(at, at, nsend.at[j, slot], nrecv.at[j, q], {"node": flip(b)})

    def n_wait(j, q):
        n_copy(j, q, 0, 0).wait_recv()

    def hops(action, d):
        j = lax.rem(w + d, n_wide)
        slot = 0
        for b in reversed(range(bits)):
            for q in held_at(b):
                action(j, q, b, slot)
                slot += 1

    for k in range(chunks):
        both_ways(0, z_begin(k))
    for d in range(1, n_wide):
        ids_copy(w, d, lax.rem(w + d, n_wide)).start()
    for d in range(1, n_wide - 1):
        for k in range(chunks):
            both_ways(d, z_pass(k))
    both_ways(0, x_begin)
    for t in range(2):
        load(t).start()
        keep(t).start()

    for d in range(1, n_wide):
        j = lax.rem(w + d, n_wide)
        ids_copy(j, d, j).wait_recv()
    ids_in = pltpu.make_async_copy(all_ids, ids_now, lsem.at[1])
    ids_in.start()
    ids_in.wait()
    number = lax.broadcasted_iota(jnp.int32, (8, EDGE), 0) * EDGE + lax.broadcasted_iota(jnp.int32, (8, EDGE), 1)

    def add_ids(j, found):
        for s in range(slots):
            hit = jnp.maximum(1 - jnp.abs(number - ids_now[j, 0, s]), 0)
            found = jnp.minimum(found, none + hit * (j * slots + s - none))
        return found

    inv_vec[...] = lax.fori_loop(0, n_wide, add_ids, jnp.full((8, EDGE), none, jnp.int32))
    inv_in = pltpu.make_async_copy(inv_vec, inv_ref, lsem.at[2])
    inv_in.start()
    inv_in.wait()

    for k in range(chunks):
        both_ways(n_wide - 1, z_pass(k))
    for d in range(1, n_wide):
        for k in range(chunks):
            y_copy(lax.rem(w + d, n_wide), k, other).wait_recv()
    own_tiles.wait()

    def place(r, _):
        for m in range(3):
            for c in range(COLS):
                b = m * per + r * COLS + c
                i = inv_ref[b // EDGE, b % EDGE]
                weights[m, pl.ds(pl.multiple_of(r * EDGE, EDGE), EDGE), c * EDGE:(c + 1) * EDGE] = blocks[i]
        return 0

    lax.fori_loop(0, rblocks, place, 0)
    both_ways(1, x_pass)

    load(0).wait()
    load(1).wait()
    gate = jnp.dot(tok_now[...], weights[0], preferred_element_type=jnp.float32)
    up = jnp.dot(tok_now[...], weights[1], preferred_element_type=jnp.float32)
    value, slope = gelu_parts(gate)
    hidden = (value * up).astype(jnp.bfloat16)
    hidden_grad = jnp.dot(cot_now[...], weights[2], preferred_element_type=jnp.float32)
    gate_grad = (hidden_grad * up * slope).astype(jnp.bfloat16)
    up_grad = (hidden_grad * value).astype(jnp.bfloat16)
    acts[0] = gate_grad
    acts[1] = up_grad
    acts[2] = hidden
    keep_acts = pltpu.make_async_copy(acts, acts_ref.at[:, own_rows, :], ssem.at[2])
    keep_acts.start()

    def h_copy(j, way, own=False):
        at = acts_ref.at[:, pl.ds(pl.multiple_of(j * toks, 16), toks), :]
        return remote(
            acts if own else at, at, hsend.at[0 if way > 0 else 1, j], hrecv.at[j], {"wide": w + way}
        )

    def h_begin(j, way, have, more):
        @pl.when(more)
        def _():
            h_copy(j, way, True).start()

    def h_pass(j, way, have, more):
        @pl.when(have)
        def _():
            h_copy(j, way).wait_recv()

        @pl.when(have & more)
        def _():
            h_copy(j, way).start()

    def h_sent(j, way, have, more):
        @pl.when(have & more)
        def _():
            h_copy(j, way).wait_send()

    both_ways(0, h_begin)

    def p_copy(t, src, to, d):
        return remote(
            parts.at[t, pl.ds(pl.multiple_of(to * piece, 16), piece), :], arrived.at[t, src],
            psend.at[t, d], precv.at[t, src], {"node": to},
        )

    out_part = contract_rows(hidden, weights[2])
    parts[0] = out_part.astype(jnp.bfloat16)
    for d in range(1, n_node):
        p_copy(0, n, lax.rem(n + d, n_node), d).start()
    if n_wide > 2:
        both_ways(2, x_pass)
    parts[1] = (contract_rows(gate_grad, weights[0]) + contract_rows(up_grad, weights[1])).astype(jnp.bfloat16)
    for d in range(1, n_node):
        p_copy(1, n, lax.rem(n + d, n_node), d).start()

    out_refs = (mixed_ref, input_ref)

    def o_copy(t, src, to, d):
        at = out_refs[t].at[pl.ds(pl.multiple_of(src * piece, 16), piece), :]
        return remote(at, at, osend.at[t, d], orecv.at[t, src], {"node": to})

    def reduce_part(t):
        mine = pl.ds(pl.multiple_of(n * piece, 16), piece)
        acc = parts[t, mine, :].astype(jnp.float32)
        for d in range(1, n_node):
            src = lax.rem(n + d, n_node)
            p_copy(t, src, src, d).wait_recv()
            acc = acc + arrived[t, src].astype(jnp.float32)
        out_refs[t][mine, :] = acc.astype(jnp.bfloat16)
        for d in range(1, n_node):
            o_copy(t, n, lax.rem(n + d, n_node), d).start()

    both_ways(1, h_pass)
    reduce_part(0)
    for d in range(3, n_wide):
        both_ways(d, x_pass)
        both_ways(d - 1, h_pass)
    reduce_part(1)
    for d in range(1, n_wide):
        j = lax.rem(w + d, n_wide)
        slot = 1
        for b in reversed(range(bits - 1)):
            held = held_at(b)
            for q in held:
                @pl.when(lax.rem(q // (1 << (b + 1)), 2) != lax.rem(n // (1 << (b + 1)), 2))
                def _():
                    n_wait(j, q)
            for q in held:
                n_copy(j, q, b, slot).start()
                slot += 1
    last = [2 * i for i in range(n_node // 2)]
    for d in range(1, n_wide):
        j = lax.rem(w + d, n_wide)
        for i in last:
            n_wait(j, i + (1 - n % 2))
    both_ways(n_wide - 1, h_pass)

    for t in range(2):
        for d in range(1, n_node):
            src = lax.rem(n + d, n_node)
            o_copy(t, src, src, d).wait_recv()
            o_copy(t, n, src, d).wait_send()
            p_copy(t, n, src, d).wait_send()
    for d in range(1, n_wide):
        hops(lambda j, q, b, slot: n_copy(j, q, b, slot).wait_send(), d)


    for d in range(n_wide):
        both_ways(d, x_sent)
        both_ways(d, h_sent)
        both_ways(d, z_sent)
    for d in range(1, n_wide):
        j = lax.rem(w + d, n_wide)
        ids_copy(w, d, j).wait_send()
        for k in range(chunks):
            y_copy(j, k, g).wait_send()
    keep(0).wait()
    keep(1).wait()
    keep_acts.wait()


def main_call(ids, tokens, cotangent, tiles, n_wide, n_node):
    toks, width = tokens.shape
    dma = pltpu.SemaphoreType.DMA
    vmem = pl.BlockSpec(memory_space=pltpu.VMEM)
    slots = tiles.shape[0]
    chunks = 5 if slots % 5 == 0 else 1
    hbm = pl.BlockSpec(memory_space=pl.ANY)
    bf16 = jnp.bfloat16
    return pl.pallas_call(
        functools.partial(main_kernel, n_wide, n_node, chunks),
        out_shape=(
            jax.ShapeDtypeStruct((toks, width), bf16),
            jax.ShapeDtypeStruct((toks, width), bf16),
            jax.ShapeDtypeStruct((2, n_wide * toks, width), bf16),
            jax.ShapeDtypeStruct((3, n_wide * toks, FF_DEV), bf16),
        ),
        in_specs=[vmem, hbm, hbm, hbm],
        out_specs=(vmem, vmem, hbm, hbm),
        scratch_shapes=[
            pltpu.VMEM((n_wide * slots + 1, EDGE, EDGE), bf16),
            pltpu.VMEM((n_wide, 8, EDGE), jnp.int32),
            pltpu.SMEM((n_wide, 8, EDGE), jnp.int32),
            pltpu.VMEM((8, EDGE), jnp.int32),
            pltpu.SMEM((8, EDGE), jnp.int32),
            pltpu.VMEM((toks, width), bf16),
            pltpu.VMEM((toks, width), bf16),
            pltpu.VMEM((3, width, FF_DEV), bf16),
            pltpu.VMEM((3, toks, FF_DEV), bf16),
            pltpu.VMEM((2, toks, width), bf16),
            pltpu.VMEM((2, n_node, toks // n_node, width), bf16),
            dma((2, n_wide, chunks)), dma((n_wide, chunks)), dma((n_wide, chunks)), dma((n_wide, chunks)),
            dma((n_wide,)), dma((n_wide,)), dma((5,)),
            dma((2, n_wide, 2)), dma((n_wide, 2)), dma((n_wide, n_node)), dma((n_wide, n_node)),
            dma((2, n_wide)), dma((n_wide,)), dma((2, n_node)), dma((2, n_node)), dma((2, n_node)), dma((2, n_node)),
            dma((3,)),
        ],
        compiler_params=pltpu.CompilerParams(
            collective_id=1, has_side_effects=True, vmem_limit_bytes=60 << 20
        ),
    )(ids, tokens, cotangent, tiles)


def grads_kernel(slots, rblocks, mine_ref, x_ref, acts_ref, out_ref, total):
    step = pl.program_id(0)
    per = rblocks * COLS

    @pl.when(step == 0)
    def _():
        total[...] = jnp.zeros_like(total)

    for s in range(slots):
        b = jnp.maximum(mine_ref[s], 0)
        m = b // per
        r = pl.multiple_of(((b // COLS) % rblocks) * EDGE, EDGE)
        c = pl.multiple_of((b % COLS) * EDGE, EDGE)
        total[s] += contract_tokens(x_ref[m // 2, :, pl.ds(r, EDGE)], acts_ref[m, :, pl.ds(c, EDGE)])

    @pl.when(step == pl.num_programs(0) - 1)
    def _():
        for s in range(slots):
            out_ref[s] = jnp.where(mine_ref[s] >= 0, total[s], 0.0).astype(out_ref.dtype)


def slot_grads(mine, gathered, acts, toks):
    slots = mine.shape[0]
    width = gathered.shape[2]
    return pl.pallas_call(
        functools.partial(grads_kernel, slots, width // EDGE),
        out_shape=jax.ShapeDtypeStruct((slots, EDGE, EDGE), jnp.bfloat16),
        grid_spec=pltpu.PrefetchScalarGridSpec(
            num_scalar_prefetch=1,
            grid=(gathered.shape[1] // toks,),
            in_specs=[
                pl.BlockSpec((2, toks, width), lambda j, ids: (0, j, 0)),
                pl.BlockSpec((3, toks, FF_DEV), lambda j, ids: (0, j, 0)),
            ],
            out_specs=pl.BlockSpec((slots, EDGE, EDGE), lambda j, ids: (0, 0, 0)),
            scratch_shapes=[pltpu.VMEM((slots, EDGE, EDGE), jnp.float32)],
        ),
        compiler_params=pltpu.CompilerParams(vmem_limit_bytes=60 << 20),
    )(mine, gathered, acts)


def per_device(n_wide, n_node, tokens, cotangent, tiles, tile_ids, tile_counts):
    slots = tiles.shape[2]
    ids = tile_ids.reshape(slots)
    mine = jnp.where(jnp.arange(slots, dtype=jnp.int32) < tile_counts[0, 0], ids, -1)
    padded = jnp.broadcast_to(jnp.pad(mine, (0, EDGE - slots), constant_values=-1)[None, :], (8, EDGE))
    mixed, input_grad, all_x, all_acts = main_call(
        padded, tokens, cotangent, tiles.reshape(slots, EDGE, EDGE), n_wide, n_node
    )
    grads = slot_grads(mine, all_x, all_acts, tokens.shape[0])
    return mixed, input_grad, grads[None, None]


def solution(mesh):
    return jax.shard_map(
        functools.partial(per_device, mesh.shape["wide"], mesh.shape["node"]),
        mesh=mesh,
        in_specs=(
            P(("groups", "wide"), None),
            P(("groups", "wide"), None),
            P("node", "wide", None, None, None),
            P("node", "wide", None),
            P("node", "wide"),
        ),
        out_specs=(
            P(("groups", "wide"), None),
            P(("groups", "wide"), None),
            P(("groups", "node"), "wide", None, None, None),
        ),
        check_vma=False,
    )
```

```python
import functools
import math

import jax
import jax.numpy as jnp
from jax import lax
from jax.experimental import pallas as pl
from jax.experimental.pallas import tpu as pltpu
from jax.sharding import PartitionSpec as P

FF_DEV = 512
EDGE = 128
COLS = FF_DEV // EDGE
MESH = pl.DeviceIdType.MESH

gelu_scale = math.sqrt(2.0 / math.pi)
cubic_term = 0.044715


def gelu_parts(pre):
    tangent = jnp.tanh(gelu_scale * (pre + cubic_term * pre * pre * pre))
    value = 0.5 * pre * (1.0 + tangent)
    slope = 0.5 * (1.0 + tangent) + 0.5 * pre * (1.0 - tangent * tangent) * gelu_scale * (
        1.0 + 3.0 * cubic_term * pre * pre
    )
    return (value, slope)


def contract_rows(left, right):
    return lax.dot_general(
        left, right, (((1,), (1,)), ((), ())), preferred_element_type=jnp.float32
    )


def contract_tokens(left, right):
    return lax.dot_general(
        left, right, (((0,), (0,)), ((), ())), preferred_element_type=jnp.float32
    )


def remote(src, dst, send, recv, where):
    return pltpu.make_async_remote_copy(
        src_ref=src, dst_ref=dst, send_sem=send, recv_sem=recv, device_id=where, device_id_type=MESH
    )


def main_kernel(n_wide, n_node, chunks,
                ids_ref, tok_ref, cot_ref, tiles_ref,
                mixed_ref, input_ref, gath_ref, acts_ref,
                blocks, all_ids, ids_now, inv_vec, inv_ref, tok_now, cot_now, weights, acts, parts, arrived,
                zsend, zrecv, ysend, yrecv, isend, irecv, lsem,
                xsend, xrecv, nsend, nrecv, hsend, hrecv, psend, precv, osend, orecv, ssem):
    w = lax.axis_index("wide")
    n = lax.axis_index("node")
    g = lax.axis_index("groups")
    other = 1 - g
    slots = tiles_ref.shape[0]
    step = slots // chunks
    none = n_wide * slots
    toks, width = tok_ref.shape
    piece = toks // n_node
    rblocks = width // EDGE
    per = rblocks * COLS
    bits = n_node.bit_length() - 1

    barrier = pltpu.get_barrier_semaphore()
    for d in range(1, n_wide):
        pl.semaphore_signal(barrier, inc=1, device_id={"wide": lax.rem(w + d, n_wide)}, device_id_type=MESH)
    for d in range(1, n_node):
        pl.semaphore_signal(barrier, inc=1, device_id={"node": lax.rem(n + d, n_node)}, device_id_type=MESH)

    pl.semaphore_signal(barrier, inc=1, device_id={"groups": other}, device_id_type=MESH)
    own_tiles = pltpu.make_async_copy(tiles_ref, blocks.at[pl.ds(w * slots, slots)], lsem.at[0])
    own_tiles.start()
    blocks[none] = jnp.zeros((EDGE, EDGE), blocks.dtype)
    all_ids[w] = ids_ref[...]

    def rows_of(j, q):
        return pl.ds(pl.multiple_of(j * toks + q * piece, 16), piece)

    own_rows = pl.ds(pl.multiple_of(w * toks, 16), toks)
    def keep(t):
        return pltpu.make_async_copy((tok_ref, cot_ref)[t], gath_ref.at[t, own_rows, :], ssem.at[t])

    def load(t):
        return pltpu.make_async_copy((tok_ref, cot_ref)[t], (tok_now, cot_now)[t], lsem.at[3 + t])

    pl.semaphore_wait(barrier, n_wide + n_node - 1)

    def both_ways(d, action):
        for way in (1, -1):
            j = w - d * way
            have = (j >= 0) if way > 0 else (j < n_wide)
            more = (w < n_wide - 1) if way > 0 else (w > 0)
            action(j, way, have, more)

    half = EDGE // 2

    def piece_of(j, group, k):
        return blocks.at[pl.ds(j * slots + k * step, step), pl.ds(pl.multiple_of(group * half, half), half), :]

    def z_copy(j, k, way, own=False):
        mine = tiles_ref.at[pl.ds(k * step, step), pl.ds(pl.multiple_of(g * half, half), half), :]
        to = piece_of(j, g, k)
        return remote(
            mine if own else to, to, zsend.at[0 if way > 0 else 1, j, k], zrecv.at[j, k], {"wide": w + way}
        )

    def y_copy(j, k, group):
        at = piece_of(j, group, k)
        return remote(at, at, ysend.at[j, k], yrecv.at[j, k], {"groups": other})

    def ids_copy(j, d, to):
        return remote(all_ids.at[j], all_ids.at[j], isend.at[d], irecv.at[j], {"wide": to})

    def z_pass(k):
        def go(j, way, have, more):
            @pl.when(have)
            def _():
                z_copy(j, k, way).wait_recv()

            @pl.when(have & more)
            def _():
                z_copy(j, k, way).start()

            @pl.when(have)
            def _():
                y_copy(j, k, g).start()
        return go

    def z_sent(j, way, have, more):
        @pl.when(have & more)
        def _():
            for k in range(chunks):
                z_copy(j, k, way).wait_send()

    def z_begin(k):
        def go(j, way, have, more):
            @pl.when(more)
            def _():
                z_copy(j, k, way, True).start()
        return go

    def x_copy(j, way, t, own=False):
        to = gath_ref.at[t, rows_of(j, n), :]
        mine = (tok_ref, cot_ref)[t].at[pl.ds(pl.multiple_of(n * piece, 16), piece), :]
        return remote(
            mine if own else to, to, xsend.at[0 if way > 0 else 1, j, t], xrecv.at[j, t], {"wide": w + way}
        )

    def x_begin(j, way, have, more):
        @pl.when(more)
        def _():
            for t in range(2):
                x_copy(j, way, t, True).start()

    def x_pass(j, way, have, more):
        @pl.when(have)
        def _():
            for t in range(2):
                x_copy(j, way, t).wait_recv()

        @pl.when(have & more)
        def _():
            for t in range(2):
                x_copy(j, way, t).start()

        @pl.when(have)
        def _():
            n_copy(j, n, bits - 1, 0).start()

    def x_sent(j, way, have, more):
        @pl.when(have & more)
        def _():
            for t in range(2):
                x_copy(j, way, t).wait_send()

    def flip(b):
        bit = lax.rem(n // (1 << b), 2)
        return n + (1 - 2 * bit) * (1 << b)

    def held_at(b):
        base = n % (1 << (b + 1))
        return [base + i * (1 << (b + 1)) for i in range(n_node >> (b + 1))]

    def n_copy(j, q, b, slot):
        at = gath_ref.at[:, rows_of(j, q), :]
        return remote(at, at, nsend.at[j, slot], nrecv.at[j, q], {"node": flip(b)})

    def n_wait(j, q):
        n_copy(j, q, 0, 0).wait_recv()

    def hops(action, d):
        j = lax.rem(w + d, n_wide)
        slot = 0
        for b in reversed(range(bits)):
            for q in held_at(b):
                action(j, q, b, slot)
                slot += 1

    for k in range(chunks):
        both_ways(0, z_begin(k))
    for d in range(1, n_wide):
        ids_copy(w, d, lax.rem(w + d, n_wide)).start()
    for d in range(1, n_wide - 1):
        for k in range(chunks):
            both_ways(d, z_pass(k))
    both_ways(0, x_begin)
    for t in range(2):
        load(t).start()
        keep(t).start()

    for d in range(1, n_wide):
        j = lax.rem(w + d, n_wide)
        ids_copy(j, d, j).wait_recv()
    ids_in = pltpu.make_async_copy(all_ids, ids_now, lsem.at[1])
    ids_in.start()
    ids_in.wait()
    number = lax.broadcasted_iota(jnp.int32, (8, EDGE), 0) * EDGE + lax.broadcasted_iota(jnp.int32, (8, EDGE), 1)

    def add_ids(j, found):
        for s in range(slots):
            hit = jnp.maximum(1 - jnp.abs(number - ids_now[j, 0, s]), 0)
            found = jnp.minimum(found, none + hit * (j * slots + s - none))
        return found

    inv_vec[...] = lax.fori_loop(0, n_wide, add_ids, jnp.full((8, EDGE), none, jnp.int32))
    inv_in = pltpu.make_async_copy(inv_vec, inv_ref, lsem.at[2])
    inv_in.start()
    inv_in.wait()

    for k in range(chunks):
        both_ways(n_wide - 1, z_pass(k))
    for d in range(1, n_wide):
        for k in range(chunks):
            y_copy(lax.rem(w + d, n_wide), k, other).wait_recv()
    own_tiles.wait()

    def place(r, _):
        for m in range(3):
            for c in range(COLS):
                b = m * per + r * COLS + c
                i = inv_ref[b // EDGE, b % EDGE]
                weights[m, pl.ds(pl.multiple_of(r * EDGE, EDGE), EDGE), c * EDGE:(c + 1) * EDGE] = blocks[i]
        return 0

    lax.fori_loop(0, rblocks, place, 0)
    both_ways(1, x_pass)

    load(0).wait()
    load(1).wait()
    gate = jnp.dot(tok_now[...], weights[0], preferred_element_type=jnp.float32)
    up = jnp.dot(tok_now[...], weights[1], preferred_element_type=jnp.float32)
    value, slope = gelu_parts(gate)
    hidden = (value * up).astype(jnp.bfloat16)
    hidden_grad = jnp.dot(cot_now[...], weights[2], preferred_element_type=jnp.float32)
    gate_grad = (hidden_grad * up * slope).astype(jnp.bfloat16)
    up_grad = (hidden_grad * value).astype(jnp.bfloat16)
    acts[0] = gate_grad
    acts[1] = up_grad
    acts[2] = hidden
    keep_acts = pltpu.make_async_copy(acts, acts_ref.at[:, own_rows, :], ssem.at[2])
    keep_acts.start()

    def h_copy(j, way, own=False):
        at = acts_ref.at[:, pl.ds(pl.multiple_of(j * toks, 16), toks), :]
        return remote(
            acts if own else at, at, hsend.at[0 if way > 0 else 1, j], hrecv.at[j], {"wide": w + way}
        )

    def h_begin(j, way, have, more):
        @pl.when(more)
        def _():
            h_copy(j, way, True).start()

    def h_pass(j, way, have, more):
        @pl.when(have)
        def _():
            h_copy(j, way).wait_recv()

        @pl.when(have & more)
        def _():
            h_copy(j, way).start()

    def h_sent(j, way, have, more):
        @pl.when(have & more)
        def _():
            h_copy(j, way).wait_send()

    both_ways(0, h_begin)

    def p_copy(t, src, to, d):
        return remote(
            parts.at[t, pl.ds(pl.multiple_of(to * piece, 16), piece), :], arrived.at[t, src],
            psend.at[t, d], precv.at[t, src], {"node": to},
        )

    out_part = contract_rows(hidden, weights[2])
    parts[0] = out_part.astype(jnp.bfloat16)
    for d in range(1, n_node):
        p_copy(0, n, lax.rem(n + d, n_node), d).start()
    if n_wide > 2:
        both_ways(2, x_pass)
    parts[1] = (contract_rows(gate_grad, weights[0]) + contract_rows(up_grad, weights[1])).astype(jnp.bfloat16)
    for d in range(1, n_node):
        p_copy(1, n, lax.rem(n + d, n_node), d).start()

    out_refs = (mixed_ref, input_ref)

    def o_copy(t, q, b, slot):
        at = out_refs[t].at[pl.ds(pl.multiple_of(q * piece, 16), piece), :]
        return remote(at, at, osend.at[t, slot], orecv.at[t, q], {"node": flip(b)})

    def reduce_part(t):
        mine = pl.ds(pl.multiple_of(n * piece, 16), piece)
        acc = parts[t, mine, :].astype(jnp.float32)
        for d in range(1, n_node):
            src = lax.rem(n + d, n_node)
            p_copy(t, src, src, d).wait_recv()
            acc = acc + arrived[t, src].astype(jnp.float32)
        out_refs[t][mine, :] = acc.astype(jnp.bfloat16)
        o_copy(t, n, bits - 1, 0).start()

    both_ways(1, h_pass)
    for d in range(3, n_wide):
        both_ways(d, x_pass)
        both_ways(d - 1, h_pass)
    reduce_part(0)
    reduce_part(1)
    for t in range(2):
        slot = 1
        for b in reversed(range(bits - 1)):
            held = held_at(b)
            for q in held:
                @pl.when(lax.rem(q // (1 << (b + 1)), 2) != lax.rem(n // (1 << (b + 1)), 2))
                def _():
                    o_copy(t, q, b, slot).wait_recv()
            for q in held:
                o_copy(t, q, b, slot).start()
                slot += 1
    for d in range(1, n_wide):
        j = lax.rem(w + d, n_wide)
        slot = 1
        for b in reversed(range(bits - 1)):
            held = held_at(b)
            for q in held:
                @pl.when(lax.rem(q // (1 << (b + 1)), 2) != lax.rem(n // (1 << (b + 1)), 2))
                def _():
                    n_wait(j, q)
            for q in held:
                n_copy(j, q, b, slot).start()
                slot += 1
    last = [2 * i for i in range(n_node // 2)]
    for d in range(1, n_wide):
        j = lax.rem(w + d, n_wide)
        for i in last:
            n_wait(j, i + (1 - n % 2))
    both_ways(n_wide - 1, h_pass)

    for t in range(2):
        for d in range(1, n_node):
            src = lax.rem(n + d, n_node)
            p_copy(t, n, src, d).wait_send()
        for i in last:
            o_copy(t, i + (1 - n % 2), 0, 0).wait_recv()
        slot = 0
        for b in reversed(range(bits)):
            for q in held_at(b):
                o_copy(t, q, b, slot).wait_send()
                slot += 1
    for d in range(1, n_wide):
        hops(lambda j, q, b, slot: n_copy(j, q, b, slot).wait_send(), d)


    for d in range(n_wide):
        both_ways(d, x_sent)
        both_ways(d, h_sent)
        both_ways(d, z_sent)
    for d in range(1, n_wide):
        j = lax.rem(w + d, n_wide)
        ids_copy(w, d, j).wait_send()
        for k in range(chunks):
            y_copy(j, k, g).wait_send()
    keep(0).wait()
    keep(1).wait()
    keep_acts.wait()


def main_call(ids, tokens, cotangent, tiles, n_wide, n_node):
    toks, width = tokens.shape
    dma = pltpu.SemaphoreType.DMA
    vmem = pl.BlockSpec(memory_space=pltpu.VMEM)
    slots = tiles.shape[0]
    chunks = 5 if slots % 5 == 0 else 1
    hbm = pl.BlockSpec(memory_space=pl.ANY)
    bf16 = jnp.bfloat16
    return pl.pallas_call(
        functools.partial(main_kernel, n_wide, n_node, chunks),
        out_shape=(
            jax.ShapeDtypeStruct((toks, width), bf16),
            jax.ShapeDtypeStruct((toks, width), bf16),
            jax.ShapeDtypeStruct((2, n_wide * toks, width), bf16),
            jax.ShapeDtypeStruct((3, n_wide * toks, FF_DEV), bf16),
        ),
        in_specs=[vmem, hbm, hbm, hbm],
        out_specs=(vmem, vmem, hbm, hbm),
        scratch_shapes=[
            pltpu.VMEM((n_wide * slots + 1, EDGE, EDGE), bf16),
            pltpu.VMEM((n_wide, 8, EDGE), jnp.int32),
            pltpu.SMEM((n_wide, 8, EDGE), jnp.int32),
            pltpu.VMEM((8, EDGE), jnp.int32),
            pltpu.SMEM((8, EDGE), jnp.int32),
            pltpu.VMEM((toks, width), bf16),
            pltpu.VMEM((toks, width), bf16),
            pltpu.VMEM((3, width, FF_DEV), bf16),
            pltpu.VMEM((3, toks, FF_DEV), bf16),
            pltpu.VMEM((2, toks, width), bf16),
            pltpu.VMEM((2, n_node, toks // n_node, width), bf16),
            dma((2, n_wide, chunks)), dma((n_wide, chunks)), dma((n_wide, chunks)), dma((n_wide, chunks)),
            dma((n_wide,)), dma((n_wide,)), dma((5,)),
            dma((2, n_wide, 2)), dma((n_wide, 2)), dma((n_wide, n_node)), dma((n_wide, n_node)),
            dma((2, n_wide)), dma((n_wide,)), dma((2, n_node)), dma((2, n_node)), dma((2, n_node)), dma((2, n_node)),
            dma((3,)),
        ],
        compiler_params=pltpu.CompilerParams(
            collective_id=1, has_side_effects=True, vmem_limit_bytes=60 << 20
        ),
    )(ids, tokens, cotangent, tiles)


def grads_kernel(slots, rblocks, mine_ref, x_ref, acts_ref, out_ref, total):
    step = pl.program_id(0)
    per = rblocks * COLS

    @pl.when(step == 0)
    def _():
        total[...] = jnp.zeros_like(total)

    for s in range(slots):
        b = jnp.maximum(mine_ref[s], 0)
        m = b // per
        r = pl.multiple_of(((b // COLS) % rblocks) * EDGE, EDGE)
        c = pl.multiple_of((b % COLS) * EDGE, EDGE)
        total[s] += contract_tokens(x_ref[m // 2, :, pl.ds(r, EDGE)], acts_ref[m, :, pl.ds(c, EDGE)])

    @pl.when(step == pl.num_programs(0) - 1)
    def _():
        for s in range(slots):
            out_ref[s] = jnp.where(mine_ref[s] >= 0, total[s], 0.0).astype(out_ref.dtype)


def slot_grads(mine, gathered, acts, toks):
    slots = mine.shape[0]
    width = gathered.shape[2]
    return pl.pallas_call(
        functools.partial(grads_kernel, slots, width // EDGE),
        out_shape=jax.ShapeDtypeStruct((slots, EDGE, EDGE), jnp.bfloat16),
        grid_spec=pltpu.PrefetchScalarGridSpec(
            num_scalar_prefetch=1,
            grid=(gathered.shape[1] // toks,),
            in_specs=[
                pl.BlockSpec((2, toks, width), lambda j, ids: (0, j, 0)),
                pl.BlockSpec((3, toks, FF_DEV), lambda j, ids: (0, j, 0)),
            ],
            out_specs=pl.BlockSpec((slots, EDGE, EDGE), lambda j, ids: (0, 0, 0)),
            scratch_shapes=[pltpu.VMEM((slots, EDGE, EDGE), jnp.float32)],
        ),
        compiler_params=pltpu.CompilerParams(vmem_limit_bytes=60 << 20),
    )(mine, gathered, acts)


def per_device(n_wide, n_node, tokens, cotangent, tiles, tile_ids, tile_counts):
    slots = tiles.shape[2]
    ids = tile_ids.reshape(slots)
    mine = jnp.where(jnp.arange(slots, dtype=jnp.int32) < tile_counts[0, 0], ids, -1)
    padded = jnp.broadcast_to(jnp.pad(mine, (0, EDGE - slots), constant_values=-1)[None, :], (8, EDGE))
    mixed, input_grad, all_x, all_acts = main_call(
        padded, tokens, cotangent, tiles.reshape(slots, EDGE, EDGE), n_wide, n_node
    )
    grads = slot_grads(mine, all_x, all_acts, tokens.shape[0])
    return mixed, input_grad, grads[None, None]


def solution(mesh):
    return jax.shard_map(
        functools.partial(per_device, mesh.shape["wide"], mesh.shape["node"]),
        mesh=mesh,
        in_specs=(
            P(("groups", "wide"), None),
            P(("groups", "wide"), None),
            P("node", "wide", None, None, None),
            P("node", "wide", None),
            P("node", "wide"),
        ),
        out_specs=(
            P(("groups", "wide"), None),
            P(("groups", "wide"), None),
            P(("groups", "node"), "wide", None, None, None),
        ),
        check_vma=False,
    )
```
